512 devices in a mesh: tile: 64 (over y_lo, z, core), dgrp: 8 (over y_hi, x).
Axes of the slice: x: 4, y: 4 (y_hi: 2, y_lo: 2; y = y_hi * 2 + y_lo), z: 16, core: 2. Of those that a mesh axis runs over, the one named last changes fastest.
Arguments:
- prediction_state: bfloat16 [8, 512, 1024], P(None, 'tile'), may hold values from -6 to 6
- hindcast_store: bfloat16 [64, 8, 512, 1024], P('dgrp', None, 'tile'), may hold values from -6 to 6
- verifying_truth: bfloat16 [64, 512, 1024], P('dgrp', 'tile'), may hold values from -6 to 6
- quantity_factor: float32 [8], replicated, may hold values from 0.03 to 0.4
- tile_day_choices: int32 [64, 48], replicated, may hold values from 0 to 63, as said below
- filled_lengths: int32 [64], replicated, may hold values from 16 to 48
Outputs:
- analog: float32 [512, 1024], P('dgrp', 'tile')
The draws below stay inside these ranges and needn't reach their ends.
Inputs may be any that keep to these rules, and one draw needn't show every extreme that they name: `tile_day_choices`: each row holds distinct dates; only the first filled_lengths entries of a row are used.
All inputs are finite; a program needn't handle non-finite values.
Results may differ from the reference program's by a relative error of at most 0.00035.
Values may be sent and summed in bfloat16 or wider, within the bound.
No kernel may reach another device: no remote copies, remote signals or barrier semaphores. Data moves between devices by JAX's collectives and lax.ppermute only.
A program may use at most 64 MiB of HBM per device.

```python
import math
import jax
import jax.numpy as jnp
from jax import lax

PREDICTED_QTYS = 8
POOL_DAYS = 64
MAXC = 48
MINC = 16
TW = 16
NTILES = 64
MERIDIAN_LINES = 512
PARALLEL_LINES = 1024


def draw_tile_day_choices(key, part):
    key = jax.random.fold_in(key, 11)
    keys = jax.random.split(key, NTILES)
    lists = jax.vmap(lambda k: jax.random.permutation(k, POOL_DAYS)[:MAXC])(keys)
    return lists.astype(jnp.int32)


def draw_filled_lengths(key, part):
    key = jax.random.fold_in(key, 23)
    first, second = jax.random.split(key)
    filled_lengths = jax.random.randint(first, (NTILES,), MINC, MAXC + 1)
    where = jax.random.randint(second, (), 0, NTILES)
    filled_lengths = filled_lengths.at[where].set(MAXC)
    filled_lengths = filled_lengths.at[(where + 1) % NTILES].set(MINC)
    return filled_lengths.astype(jnp.int32)


def steps_of(stream_key, shape, cuts, low, largest):
    loudness = 1.0
    for axis_at, shards_of in cuts:
        heights = jax.random.uniform(jax.random.fold_in(jax.random.fold_in(stream_key, 6), axis_at), (shards_of,), jnp.float32, low / len(cuts), largest / len(cuts))
        loudness = loudness * jnp.repeat(jnp.exp(heights), shape[axis_at] // shards_of).reshape((-1,) + (1,) * (len(shape) - 1 - axis_at))
    return loudness


def centred(stream_key, shape, spread, reach, cuts=(), held_as=jnp.bfloat16):
    values = spread * jax.random.normal(stream_key, shape, jnp.float32)
    if cuts:
        values = values * steps_of(stream_key, shape, cuts, -0.22, 0.18)
    return jnp.clip(values, -reach, reach).astype(held_as)


def setup_inputs(seed: int = 0) -> dict:
    key_of = jax.random.split(jax.random.key(seed), 7)
    prediction_state = centred(key_of[0], (PREDICTED_QTYS, MERIDIAN_LINES, PARALLEL_LINES), 1.0, 6.0, ((1, 64),))
    hindcast_store = centred(key_of[1], (POOL_DAYS, PREDICTED_QTYS, MERIDIAN_LINES, PARALLEL_LINES), 1.0, 6.0, ((0, 8), (2, 64)))
    verifying_truth = centred(key_of[2], (POOL_DAYS, MERIDIAN_LINES, PARALLEL_LINES), 1.0, 6.0, ((0, 8), (1, 64)))
    quantity_factor = jnp.clip(jnp.exp(jax.random.uniform(key_of[3], (PREDICTED_QTYS,), jnp.float32, math.log(0.03), math.log(0.4))), 0.03, 0.4)
    tile_day_choices = draw_tile_day_choices(jax.random.fold_in(key_of[6], 71), 0)
    filled_lengths = draw_filled_lengths(jax.random.fold_in(key_of[6], 71), 0)
    return dict(prediction_state=prediction_state, hindcast_store=hindcast_store, verifying_truth=verifying_truth, quantity_factor=quantity_factor, tile_day_choices=tile_day_choices, filled_lengths=filled_lengths)


def member_table(tile_day_choices, filled_lengths, dates):
    hit = tile_day_choices[:, :, None] == dates[None, None, :]
    live = jnp.arange(tile_day_choices.shape[1], dtype=jnp.int32)[None, :, None] < filled_lengths[:, None, None]
    return jnp.any(hit & live, axis=1).astype(jnp.float32)


def box_sum(padded):
    rows_sum = padded[..., :-2, :] + padded[..., 1:-1, :] + padded[..., 2:, :]
    return rows_sum[..., :-2] + rows_sum[..., 1:-1] + rows_sum[..., 2:]


def reference(prediction_state, hindcast_store, verifying_truth, quantity_factor, tile_day_choices, filled_lengths):
    member = member_table(tile_day_choices, filled_lengths, jnp.arange(POOL_DAYS, dtype=jnp.int32))
    predicted_quantity = prediction_state.astype(jnp.float32)

    def one_date(carry, calendar_day):
        num, den = carry
        deviation = predicted_quantity - hindcast_store[calendar_day].astype(jnp.float32)
        err = jnp.sum(quantity_factor[:, None, None] * deviation * deviation, axis=0)
        dist = box_sum(jnp.pad(err, 1)) / 9.0
        base = 1.0 / (1.0 + dist)
        squared_deviation = base * base
        column = jnp.repeat(member[:, calendar_day], TW)
        weight = squared_deviation * squared_deviation * column[None, :]
        return (num + weight * verifying_truth[calendar_day].astype(jnp.float32), den + weight), None

    start = (jnp.zeros((MERIDIAN_LINES, PARALLEL_LINES), jnp.float32), jnp.zeros((MERIDIAN_LINES, PARALLEL_LINES), jnp.float32))
    (num, den), _ = lax.scan(one_date, start, jnp.arange(POOL_DAYS, dtype=jnp.int32))
    return num / den
```

```python
import functools

import jax
import jax.numpy as jnp
from jax import lax
from jax.experimental import pallas as pl
from jax.experimental.pallas import tpu as pltpu
from jax.sharding import PartitionSpec as P

DATES, QTYS, ROWS, COLS = 8, 8, 8, 1024
TILES, TW, LANES = 64, 16, 128
MAXC = 48
GROUPS = LANES // TW


def member_rows(base, choices, filled):
    slot = lax.broadcasted_iota(jnp.int32, (MAXC, TILES), 0)
    local = jnp.where(slot < filled, choices - base, -1)
    flags = [
        jnp.sum(jnp.where(local == d, 1.0, 0.0), axis=0, keepdims=True) for d in range(DATES)
    ]
    flags = jnp.concatenate(flags, axis=0).astype(jnp.bfloat16)
    tile = lax.broadcasted_iota(jnp.int32, (TILES, COLS), 0)
    col = lax.broadcasted_iota(jnp.int32, (TILES, COLS), 1)
    spread = jnp.where(col // TW == tile, 1.0, 0.0).astype(jnp.bfloat16)
    return jnp.dot(flags, spread, preferred_element_type=jnp.float32)


def fourth(dist9):
    base = 1.0 / (1.0 + dist9 / 9.0)
    base = base * base
    return base * base


def band_kernel(
    first_date, factor, pred, hind, truth, choices, filled, out, held, shown, exact, parts, sems
):
    copies = [pltpu.make_async_copy(hind.at[d], held.at[d], sems.at[d]) for d in range(DATES)]
    seen = pltpu.make_async_copy(pred, shown, sems.at[DATES])
    seen.start()
    for copy in copies:
        copy.start()
    member = member_rows(first_date(), choices[...], filled[...])
    col = lax.broadcasted_iota(jnp.int32, (ROWS, COLS), 1)
    sub = lax.broadcasted_iota(jnp.int32, (ROWS, COLS), 0)
    seen.wait()
    exact[...] = shown[...].astype(jnp.float32)
    num = jnp.zeros((ROWS, COLS), jnp.float32)
    den = jnp.zeros((ROWS, COLS), jnp.float32)
    for d in range(DATES):
        copies[d].wait()
        err = jnp.zeros((ROWS, COLS), jnp.float32)
        for v in range(QTYS):
            dev = exact[v] - held[d, v].astype(jnp.float32)
            err = err + factor[v] * dev * dev
        left = jnp.where(col == 0, 0.0, pltpu.roll(err, 1, 1))
        right = jnp.where(col == COLS - 1, 0.0, pltpu.roll(err, COLS - 1, 1))
        side = err + left + right
        above, below = pltpu.roll(side, 1, 0), pltpu.roll(side, ROWS - 1, 0)
        flag = jnp.broadcast_to(member[d : d + 1], (ROWS, COLS))
        seen_truth = truth[d].astype(jnp.float32)
        weight = fourth(side + above + below) * flag
        num = num + weight * seen_truth
        den = den + weight
        part = jnp.where(sub == 1, jnp.where(flag > 0, side + above, -1.0), side)
        part = jnp.where(sub == 6, jnp.where(flag > 0, side + below, -1.0), part)
        part = jnp.where(sub == 2, pltpu.roll(seen_truth, 2, 0), part)
        part = jnp.where(sub == 5, pltpu.roll(seen_truth, ROWS - 2, 0), part)
        parts[d] = part
    lane = lax.broadcasted_iota(jnp.int32, (ROWS, LANES), 1) // TW
    sub = lax.broadcasted_iota(jnp.int32, (ROWS, LANES), 0)
    for j in range(COLS // LANES):
        at = slice(j * LANES, (j + 1) * LANES)
        v = []
        for d in range(DATES):
            part = parts[d, :, at]
            part = jnp.where(sub == 3, pltpu.roll(num[:, at], (3 - d) % ROWS, 0), part)
            part = jnp.where(sub == 4, pltpu.roll(den[:, at], (4 - d) % ROWS, 0), part)
            v.append(part)
        for s in (1, 2, 4):
            odd = (lane & s) != 0
            for a in range(GROUPS):
                if a & s:
                    continue
                low, high = v[a], v[a | s]
                v[a] = jnp.where(odd, pltpu.roll(high, TW * s, 1), low)
                v[a | s] = jnp.where(odd, high, pltpu.roll(low, LANES - TW * s, 1))
        for t in range(GROUPS):
            out[j * GROUPS + t] = v[t]


def band_blocks(first_date, prediction, hindcast, truth, factor, choices, filled, **kw):
    vmem = pl.BlockSpec(memory_space=pltpu.VMEM)
    hbm = pl.BlockSpec(memory_space=pl.ANY)
    return pl.pallas_call(
        functools.partial(band_kernel, first_date),
        out_shape=jax.ShapeDtypeStruct((TILES, ROWS, LANES), jnp.float32),
        in_specs=[pl.BlockSpec(memory_space=pltpu.SMEM), hbm, hbm, vmem, vmem, vmem],
        out_specs=vmem,
        scratch_shapes=[
            pltpu.VMEM((DATES, QTYS, ROWS, COLS), jnp.bfloat16),
            pltpu.VMEM((QTYS, ROWS, COLS), jnp.bfloat16),
            pltpu.VMEM((QTYS, ROWS, COLS), jnp.float32),
            pltpu.VMEM((DATES, ROWS, COLS), jnp.float32),
            pltpu.SemaphoreType.DMA((DATES + 1,)),
        ],
        compiler_params=pltpu.CompilerParams(vmem_limit_bytes=16 << 20),
        **kw,
    )(factor, prediction, hindcast, truth, choices.T, filled[None])


def lane_groups_sum(x):
    for s in (4, 2, 1):
        x = x + pltpu.roll(x, TW * s, 1)
    return x


def column_kernel(got, out):
    side0, pair0, truth0, num = got[:, 0], got[:, 1], got[:, 2], got[:, 3]
    den, truth7, pair7, side7 = got[:, 4], got[:, 5], got[:, 6], got[:, 7]
    band = lax.broadcasted_iota(jnp.int32, (TILES, LANES), 0)
    row = lax.broadcasted_iota(jnp.int32, (TILES, LANES), 1) // TW
    above = jnp.where(band == 0, 0.0, pltpu.roll(side7, 1, 0))
    below = jnp.where(band == TILES - 1, 0.0, pltpu.roll(side0, TILES - 1, 0))
    weight0 = jnp.where(pair0 < 0, 0.0, fourth(pair0 + above))
    weight7 = jnp.where(pair7 < 0, 0.0, fourth(pair7 + below))
    num = jnp.where(row == 0, lane_groups_sum(weight0 * truth0), num)
    num = jnp.where(row == ROWS - 1, lane_groups_sum(weight7 * truth7), num)
    den = jnp.where(row == 0, lane_groups_sum(weight0), den)
    den = jnp.where(row == ROWS - 1, lane_groups_sum(weight7), den)
    for g in range(8):
        out[g, 0:8] = num[8 * g : 8 * g + 8]
        out[g, 8:16] = den[8 * g : 8 * g + 8]


def column_sums(got, **kw):
    vmem = pl.BlockSpec(memory_space=pltpu.VMEM)
    return pl.pallas_call(
        column_kernel,
        out_shape=jax.ShapeDtypeStruct((8, 16, LANES), jnp.float32),
        in_specs=[vmem],
        out_specs=vmem,
        **kw,
    )(got)


def analog_kernel(sums, out):
    total = sums[0]
    for g in range(1, 8):
        total = total + sums[g]
    analog = total[0:8] / total[8:16]
    lane = lax.broadcasted_iota(jnp.int32, (8, LANES), 1)
    sub = lax.broadcasted_iota(jnp.int32, (8, LANES), 0)
    x = jnp.take_along_axis(analog, (lane % 8) * TW + lane // 8, axis=1)
    for s in (1, 2, 4):
        odd_lane, odd_sub = ((lane // 8) & s) != 0, (sub & s) != 0
        up = pltpu.roll(pltpu.roll(x, 8 - s, 0), 8 * s, 1)
        down = pltpu.roll(pltpu.roll(x, s, 0), LANES - 8 * s, 1)
        x = jnp.where(odd_lane == odd_sub, x, jnp.where(odd_lane, up, down))
    out[0:8] = x[:, 0:64]
    out[8:16] = x[:, 64:128]


def analog_block(sums, **kw):
    vmem = pl.BlockSpec(memory_space=pltpu.VMEM)
    return pl.pallas_call(
        analog_kernel,
        out_shape=jax.ShapeDtypeStruct((TW, 64), jnp.float32),
        in_specs=[vmem],
        out_specs=vmem,
        **kw,
    )(sums)


def local(
    prediction_state,
    hindcast_store,
    verifying_truth,
    quantity_factor,
    tile_day_choices,
    filled_lengths,
):
    blocks = band_blocks(
        lambda: lax.axis_index("dgrp") * DATES,
        prediction_state,
        hindcast_store,
        verifying_truth,
        quantity_factor,
        tile_day_choices,
        filled_lengths,
    )
    got = lax.all_to_all(blocks, "tile", split_axis=0, concat_axis=0, tiled=True)
    sums = column_sums(got)
    sums = lax.all_to_all(sums, "dgrp", split_axis=0, concat_axis=0, tiled=True)
    return analog_block(sums).T


def solution(mesh):
    in_specs = (
        P(None, "tile", None),
        P("dgrp", None, "tile", None),
        P("dgrp", "tile", None),
        P(),
        P(),
        P(),
    )
    out_specs = P("dgrp", "tile")
    return jax.shard_map(local, mesh=mesh, in_specs=in_specs, out_specs=out_specs, check_vma=False)
```

```python
import functools

import jax
import jax.numpy as jnp
from jax import lax
from jax.experimental import pallas as pl
from jax.experimental.pallas import tpu as pltpu
from jax.sharding import PartitionSpec as P

DATES, QTYS, ROWS, COLS = 8, 8, 8, 1024
TILES, TW, LANES = 64, 16, 128
MAXC = 48
GROUPS = LANES // TW

SQUARE_SCALE, MEAN_SCALE, TRUTH_SCALE = 2.0**-7, 2.0**10, 2.0**13
SMALL, LARGE_SCALE, SMALL_SCALE = 2.0**-26, 2.0**12, 2.0**41


def member_rows(base, choices, filled):
    slot = lax.broadcasted_iota(jnp.int32, (MAXC, TILES), 0)
    local = jnp.where(slot < filled, choices - base, -1)
    flags = [
        jnp.sum(jnp.where(local == d, 1.0, 0.0), axis=0, keepdims=True) for d in range(DATES)
    ]
    flags = jnp.concatenate(flags, axis=0).astype(jnp.bfloat16)
    tile = lax.broadcasted_iota(jnp.int32, (TILES, COLS), 0)
    col = lax.broadcasted_iota(jnp.int32, (TILES, COLS), 1)
    spread = jnp.where(col // TW == tile, 1.0, 0.0).astype(jnp.bfloat16)
    return jnp.dot(flags, spread, preferred_element_type=jnp.float32)


def fourth(dist9):
    base = 1.0 / (1.0 + dist9 / 9.0)
    base = base * base
    return base * base


def to_11_bits(x):
    c = x * (2.0**13 + 1)
    return c - (c - x)


def band_kernel(
    first_date, factor, pred, hind, truth, choices, filled, out, held, shown, exact, parts, sems
):
    copies = [pltpu.make_async_copy(hind.at[d], held.at[d], sems.at[d]) for d in range(DATES)]
    seen = pltpu.make_async_copy(pred, shown, sems.at[DATES])
    seen.start()
    for copy in copies:
        copy.start()
    member = member_rows(first_date(), choices[...], filled[...])
    col = lax.broadcasted_iota(jnp.int32, (ROWS, COLS), 1)
    sub = lax.broadcasted_iota(jnp.int32, (ROWS, COLS), 0)
    seen.wait()
    exact[...] = shown[...].astype(jnp.float32)
    num = jnp.zeros((ROWS, COLS), jnp.float32)
    den = jnp.zeros((ROWS, COLS), jnp.float32)
    for d in range(DATES):
        copies[d].wait()
        err = jnp.zeros((ROWS, COLS), jnp.float32)
        for v in range(QTYS):
            dev = exact[v] - held[d, v].astype(jnp.float32)
            err = err + factor[v] * dev * dev
        left = jnp.where(col == 0, 0.0, pltpu.roll(err, 1, 1))
        right = jnp.where(col == COLS - 1, 0.0, pltpu.roll(err, COLS - 1, 1))
        side = err + left + right
        above, below = pltpu.roll(side, 1, 0), pltpu.roll(side, ROWS - 1, 0)
        flag = jnp.broadcast_to(member[d : d + 1], (ROWS, COLS))
        seen_truth = truth[d].astype(jnp.float32)
        weight = fourth(side + above + below) * flag
        num = num + weight * seen_truth
        den = den + weight
        pair = jnp.where(sub == 1, side + above, side + below)
        pair = jnp.where(flag > 0, pair * pair * SQUARE_SCALE, -1.0)
        part = jnp.where((sub == 1) | (sub == 6), pair, side * side * SQUARE_SCALE)
        scaled = seen_truth * TRUTH_SCALE
        part = jnp.where(sub == 2, pltpu.roll(scaled, 2, 0), part)
        parts[d] = jnp.where(sub == 5, pltpu.roll(scaled, ROWS - 2, 0), part)
    high = den >= SMALL
    den = to_11_bits(jnp.where(high, den * LARGE_SCALE, den * -SMALL_SCALE))
    held_den = jnp.where(high, den * (1 / LARGE_SCALE), den * (-1 / SMALL_SCALE))
    mean = jnp.where(held_den > 0, num / held_den, 0.0)
    num = mean * jnp.abs(mean) * MEAN_SCALE
    lane = lax.broadcasted_iota(jnp.int32, (ROWS, LANES), 1) // TW
    sub = lax.broadcasted_iota(jnp.int32, (ROWS, LANES), 0)
    for j in range(COLS // LANES):
        at = slice(j * LANES, (j + 1) * LANES)
        v = []
        for d in range(DATES):
            part = parts[d, :, at]
            part = jnp.where(sub == 3, pltpu.roll(num[:, at], (3 - d) % ROWS, 0), part)
            part = jnp.where(sub == 4, pltpu.roll(den[:, at], (4 - d) % ROWS, 0), part)
            v.append(part)
        for s in (1, 2, 4):
            odd = (lane & s) != 0
            for a in range(GROUPS):
                if a & s:
                    continue
                low, high = v[a], v[a | s]
                v[a] = jnp.where(odd, pltpu.roll(high, TW * s, 1), low)
                v[a | s] = jnp.where(odd, high, pltpu.roll(low, LANES - TW * s, 1))
        for t in range(GROUPS):
            out[j * GROUPS + t] = v[t]


def band_blocks(first_date, prediction, hindcast, truth, factor, choices, filled, **kw):
    vmem = pl.BlockSpec(memory_space=pltpu.VMEM)
    hbm = pl.BlockSpec(memory_space=pl.ANY)
    return pl.pallas_call(
        functools.partial(band_kernel, first_date),
        out_shape=jax.ShapeDtypeStruct((TILES, ROWS, LANES), jnp.float32),
        in_specs=[pl.BlockSpec(memory_space=pltpu.SMEM), hbm, hbm, vmem, vmem, vmem],
        out_specs=vmem,
        scratch_shapes=[
            pltpu.VMEM((DATES, QTYS, ROWS, COLS), jnp.bfloat16),
            pltpu.VMEM((QTYS, ROWS, COLS), jnp.bfloat16),
            pltpu.VMEM((QTYS, ROWS, COLS), jnp.float32),
            pltpu.VMEM((DATES, ROWS, COLS), jnp.float32),
            pltpu.SemaphoreType.DMA((DATES + 1,)),
        ],
        compiler_params=pltpu.CompilerParams(vmem_limit_bytes=8 << 20),
        **kw,
    )(
        *(
            pltpu.with_memory_space_constraint(x, pltpu.HBM)
            for x in (factor, prediction, hindcast, truth, choices.T, filled[None])
        )
    )


def lane_groups_sum(x):
    for s in (4, 2, 1):
        x = x + pltpu.roll(x, TW * s, 1)
    return x


def column_kernel(got, out):
    side0, pair0, truth0, mean = got[:, 0], got[:, 1], got[:, 2], got[:, 3]
    den, truth7, pair7, side7 = got[:, 4], got[:, 5], got[:, 6], got[:, 7]
    dated0, dated7 = pair0 >= 0, pair7 >= 0
    side0, pair0, pair7, side7 = (
        jnp.sqrt(jnp.maximum(x, 0.0) * (1 / SQUARE_SCALE)) for x in (side0, pair0, pair7, side7)
    )
    truth0, truth7 = truth0 * (1 / TRUTH_SCALE), truth7 * (1 / TRUTH_SCALE)
    den = jnp.where(den < 0, den * (-1 / SMALL_SCALE), den * (1 / LARGE_SCALE))
    mean_size = jnp.sqrt(jnp.abs(mean) * (1 / MEAN_SCALE))
    num = jnp.where(mean < 0, -mean_size, mean_size) * den
    band = lax.broadcasted_iota(jnp.int32, (TILES, LANES), 0)
    row = lax.broadcasted_iota(jnp.int32, (TILES, LANES), 1) // TW
    above = jnp.where(band == 0, 0.0, pltpu.roll(side7, 1, 0))
    below = jnp.where(band == TILES - 1, 0.0, pltpu.roll(side0, TILES - 1, 0))
    weight0 = jnp.where(dated0, fourth(pair0 + above), 0.0)
    weight7 = jnp.where(dated7, fourth(pair7 + below), 0.0)
    num = jnp.where(row == 0, lane_groups_sum(weight0 * truth0), num)
    num = jnp.where(row == ROWS - 1, lane_groups_sum(weight7 * truth7), num)
    den = jnp.where(row == 0, lane_groups_sum(weight0), den)
    den = jnp.where(row == ROWS - 1, lane_groups_sum(weight7), den)
    for g in range(8):
        out[g, 0:8] = num[8 * g : 8 * g + 8]
        out[g, 8:16] = den[8 * g : 8 * g + 8]


def column_sums(got, **kw):
    vmem = pl.BlockSpec(memory_space=pltpu.VMEM)
    return pl.pallas_call(
        column_kernel,
        out_shape=jax.ShapeDtypeStruct((8, 16, LANES), jnp.float32),
        in_specs=[vmem],
        out_specs=vmem,
        compiler_params=pltpu.CompilerParams(vmem_limit_bytes=4 << 20),
        **kw,
    )(got)


def analog_kernel(sums, out):
    total = sums[0]
    for g in range(1, 8):
        total = total + sums[g]
    analog = total[0:8] / total[8:16]
    lane = lax.broadcasted_iota(jnp.int32, (8, LANES), 1)
    sub = lax.broadcasted_iota(jnp.int32, (8, LANES), 0)
    x = jnp.take_along_axis(analog, (lane % 8) * TW + lane // 8, axis=1)
    for s in (1, 2, 4):
        odd_lane, odd_sub = ((lane // 8) & s) != 0, (sub & s) != 0
        up = pltpu.roll(pltpu.roll(x, 8 - s, 0), 8 * s, 1)
        down = pltpu.roll(pltpu.roll(x, s, 0), LANES - 8 * s, 1)
        x = jnp.where(odd_lane == odd_sub, x, jnp.where(odd_lane, up, down))
    out[0:8] = x[:, 0:64]
    out[8:16] = x[:, 64:128]


def analog_block(sums, **kw):
    vmem = pl.BlockSpec(memory_space=pltpu.VMEM)
    return pl.pallas_call(
        analog_kernel,
        out_shape=jax.ShapeDtypeStruct((TW, 64), jnp.float32),
        in_specs=[vmem],
        out_specs=vmem,
        compiler_params=pltpu.CompilerParams(vmem_limit_bytes=4 << 20),
        **kw,
    )(sums)


def local(
    prediction_state,
    hindcast_store,
    verifying_truth,
    quantity_factor,
    tile_day_choices,
    filled_lengths,
):
    blocks = band_blocks(
        lambda: lax.axis_index("dgrp") * DATES,
        prediction_state,
        hindcast_store,
        verifying_truth,
        quantity_factor,
        tile_day_choices,
        filled_lengths,
    )
    blocks = blocks.astype(jnp.float16)
    got = lax.all_to_all(blocks, "tile", split_axis=0, concat_axis=0, tiled=True)
    sums = column_sums(got.astype(jnp.float32))
    sums = lax.all_to_all(sums, "dgrp", split_axis=0, concat_axis=0, tiled=True)
    return analog_block(sums).T


def solution(mesh):
    in_specs = (
        P(None, "tile", None),
        P("dgrp", None, "tile", None),
        P("dgrp", "tile", None),
        P(),
        P(),
        P(),
    )
    out_specs = P("dgrp", "tile")
    return jax.shard_map(local, mesh=mesh, in_specs=in_specs, out_specs=out_specs, check_vma=False)
```

```python
import functools

import jax
import jax.numpy as jnp
from jax import lax
from jax.experimental import pallas as pl
from jax.experimental.pallas import tpu as pltpu
from jax.sharding import PartitionSpec as P

DATES, QTYS, ROWS, COLS = 8, 8, 8, 1024
TILES, TW, LANES = 64, 16, 128
MAXC = 48
FIRST_TILE = 48
TILE_ORDER = [(FIRST_TILE + i) % TILES for i in range(TILES)]
GROUP_ORDER = [7, 6, 5, 4, 3, 2, 1, 0]
GROUPS = LANES // TW

SQUARE_SCALE, MEAN_SCALE, TRUTH_SCALE = 2.0**-7, 2.0**10, 2.0**13
SMALL, LARGE_SCALE, SMALL_SCALE = 2.0**-26, 2.0**12, 2.0**41


def member_rows(base, choices, filled):
    slot = lax.broadcasted_iota(jnp.int32, (MAXC, TILES), 0)
    local = jnp.where(slot < filled, choices - base, -1)
    flags = [
        jnp.sum(jnp.where(local == d, 1.0, 0.0), axis=0, keepdims=True) for d in range(DATES)
    ]
    flags = jnp.concatenate(flags, axis=0).astype(jnp.bfloat16)
    tile = lax.broadcasted_iota(jnp.int32, (TILES, COLS), 0)
    col = lax.broadcasted_iota(jnp.int32, (TILES, COLS), 1)
    spread = jnp.where(col // TW == tile, 1.0, 0.0).astype(jnp.bfloat16)
    return jnp.dot(flags, spread, preferred_element_type=jnp.float32)


def fourth(dist9):
    base = 1.0 / (1.0 + dist9 * (1 / 9.0))
    base = base * base
    return base * base


def to_11_bits(x):
    c = x * (2.0**13 + 1)
    return c - (c - x)


def band_kernel(
    first_date,
    factor_in,
    pred_in,
    hind_in,
    truth_in,
    choices_in,
    filled_in,
    out,
    factor,
    shown,
    held,
    truth,
    choices,
    filled,
    exact,
    parts,
    sems,
):
    copies = [pltpu.make_async_copy(hind_in.at[d], held.at[d], sems.at[d]) for d in range(DATES)]
    pairs = (
        (choices_in, choices),
        (filled_in, filled),
        (pred_in, shown),
        (factor_in, factor),
        (truth_in, truth),
    )
    small = [
        pltpu.make_async_copy(src, dst, sems.at[DATES + i]) for i, (src, dst) in enumerate(pairs)
    ]
    for copy in small[:4] + copies[:1] + small[4:] + copies[1:]:
        copy.start()
    small[0].wait()
    small[1].wait()
    member = member_rows(first_date(), choices[...], filled[...])
    col = lax.broadcasted_iota(jnp.int32, (ROWS, COLS), 1)
    sub = lax.broadcasted_iota(jnp.int32, (ROWS, COLS), 0)
    small[2].wait()
    exact[...] = shown[...].astype(jnp.float32)
    small[3].wait()
    small[4].wait()
    num = jnp.zeros((ROWS, COLS), jnp.float32)
    den = jnp.zeros((ROWS, COLS), jnp.float32)
    for d in range(DATES):
        copies[d].wait()
        err = jnp.zeros((ROWS, COLS), jnp.float32)
        for v in range(QTYS):
            dev = exact[v] - held[d, v].astype(jnp.float32)
            err = err + factor[v] * dev * dev
        left = jnp.where(col == 0, 0.0, pltpu.roll(err, 1, 1))
        right = jnp.where(col == COLS - 1, 0.0, pltpu.roll(err, COLS - 1, 1))
        side = err + left + right
        above, below = pltpu.roll(side, 1, 0), pltpu.roll(side, ROWS - 1, 0)
        flag = jnp.broadcast_to(member[d : d + 1], (ROWS, COLS))
        seen_truth = truth[d].astype(jnp.float32)
        weight = fourth(side + above + below) * flag
        num = num + weight * seen_truth
        den = den + weight
        pair = jnp.where(sub == 1, side + above, side + below)
        pair = jnp.where(flag > 0, pair * pair * SQUARE_SCALE, -1.0)
        part = jnp.where((sub == 1) | (sub == 6), pair, side * side * SQUARE_SCALE)
        scaled = seen_truth * TRUTH_SCALE
        part = jnp.where(sub == 2, pltpu.roll(scaled, 2, 0), part)
        parts[d] = jnp.where(sub == 5, pltpu.roll(scaled, ROWS - 2, 0), part)
    high = den >= SMALL
    den = to_11_bits(jnp.where(high, den * LARGE_SCALE, den * -SMALL_SCALE))
    held_den = jnp.where(high, den * (1 / LARGE_SCALE), den * (-1 / SMALL_SCALE))
    mean = jnp.where(held_den > 0, num / held_den, 0.0)
    num = mean * jnp.abs(mean) * MEAN_SCALE
    lane = lax.broadcasted_iota(jnp.int32, (ROWS, LANES), 1) // TW
    sub = lax.broadcasted_iota(jnp.int32, (ROWS, LANES), 0)
    for j in range(COLS // LANES):
        at = slice(j * LANES, (j + 1) * LANES)
        v = []
        for d in range(DATES):
            part = parts[d, :, at]
            part = jnp.where(sub == 3, pltpu.roll(num[:, at], (3 - d) % ROWS, 0), part)
            part = jnp.where(sub == 4, pltpu.roll(den[:, at], (4 - d) % ROWS, 0), part)
            v.append(part)
        for s in (1, 2, 4):
            odd = (lane & s) != 0
            for a in range(GROUPS):
                if a & s:
                    continue
                low, high = v[a], v[a | s]
                v[a] = jnp.where(odd, pltpu.roll(high, TW * s, 1), low)
                v[a | s] = jnp.where(odd, high, pltpu.roll(low, LANES - TW * s, 1))
        for t in range(GROUPS):
            out[(j * GROUPS + t - FIRST_TILE) % TILES] = v[t]


def band_blocks(first_date, prediction, hindcast, truth, factor, choices, filled, **kw):
    hbm = pl.BlockSpec(memory_space=pltpu.HBM)
    return pl.pallas_call(
        functools.partial(band_kernel, first_date),
        out_shape=jax.ShapeDtypeStruct((TILES, ROWS, LANES), jnp.float32),
        in_specs=[hbm] * 6,
        out_specs=pl.BlockSpec(memory_space=pltpu.VMEM),
        scratch_shapes=[
            pltpu.SMEM((QTYS,), jnp.float32),
            pltpu.VMEM((QTYS, ROWS, COLS), jnp.bfloat16),
            pltpu.VMEM((DATES, QTYS, ROWS, COLS), jnp.bfloat16),
            pltpu.VMEM((DATES, ROWS, COLS), jnp.bfloat16),
            pltpu.VMEM((MAXC, TILES), jnp.int32),
            pltpu.VMEM((1, TILES), jnp.int32),
            pltpu.VMEM((QTYS, ROWS, COLS), jnp.float32),
            pltpu.VMEM((DATES, ROWS, COLS), jnp.float32),
            pltpu.SemaphoreType.DMA((DATES + 5,)),
        ],
        compiler_params=pltpu.CompilerParams(vmem_limit_bytes=8 << 20),
        **kw,
    )(
        *(
            pltpu.with_memory_space_constraint(x, pltpu.HBM)
            for x in (factor, prediction, hindcast, truth, choices.T, filled[None])
        )
    )


def lane_groups_sum(x):
    for s in (4, 2, 1):
        x = x + pltpu.roll(x, TW * s, 1)
    return x


def column_kernel(got, out):
    side0, pair0, truth0, mean = got[:, 0], got[:, 1], got[:, 2], got[:, 3]
    den, truth7, pair7, side7 = got[:, 4], got[:, 5], got[:, 6], got[:, 7]
    dated0, dated7 = pair0 >= 0, pair7 >= 0
    side0, pair0, pair7, side7 = (
        jnp.sqrt(jnp.maximum(x, 0.0) * (1 / SQUARE_SCALE)) for x in (side0, pair0, pair7, side7)
    )
    truth0, truth7 = truth0 * (1 / TRUTH_SCALE), truth7 * (1 / TRUTH_SCALE)
    den = jnp.where(den < 0, den * (-1 / SMALL_SCALE), den * (1 / LARGE_SCALE))
    mean_size = jnp.sqrt(jnp.abs(mean) * (1 / MEAN_SCALE))
    num = jnp.where(mean < 0, -mean_size, mean_size) * den
    band = (lax.broadcasted_iota(jnp.int32, (TILES, LANES), 0) + FIRST_TILE) % TILES
    row = lax.broadcasted_iota(jnp.int32, (TILES, LANES), 1) // TW
    above = jnp.where(band == 0, 0.0, pltpu.roll(side7, 1, 0))
    below = jnp.where(band == TILES - 1, 0.0, pltpu.roll(side0, TILES - 1, 0))
    weight0 = jnp.where(dated0, fourth(pair0 + above), 0.0)
    weight7 = jnp.where(dated7, fourth(pair7 + below), 0.0)
    num = jnp.where(row == 0, lane_groups_sum(weight0 * truth0), num)
    num = jnp.where(row == ROWS - 1, lane_groups_sum(weight7 * truth7), num)
    den = jnp.where(row == 0, lane_groups_sum(weight0), den)
    den = jnp.where(row == ROWS - 1, lane_groups_sum(weight7), den)
    for place, g in enumerate(GROUP_ORDER):
        at = (8 * g - FIRST_TILE) % TILES
        out[place, 0:8] = num[at : at + 8]
        out[place, 8:16] = den[at : at + 8]


def column_sums(got, **kw):
    vmem = pl.BlockSpec(memory_space=pltpu.VMEM)
    return pl.pallas_call(
        column_kernel,
        out_shape=jax.ShapeDtypeStruct((8, 16, LANES), jnp.float32),
        in_specs=[vmem],
        out_specs=vmem,
        compiler_params=pltpu.CompilerParams(vmem_limit_bytes=4 << 20),
        **kw,
    )(got)


def analog_kernel(sums, out):
    total = sums[0]
    for g in range(1, 8):
        total = total + sums[g]
    analog = total[0:8] / total[8:16]
    lane = lax.broadcasted_iota(jnp.int32, (8, LANES), 1)
    sub = lax.broadcasted_iota(jnp.int32, (8, LANES), 0)
    x = jnp.take_along_axis(analog, (lane % 8) * TW + lane // 8, axis=1)
    for s in (1, 2, 4):
        odd_lane, odd_sub = ((lane // 8) & s) != 0, (sub & s) != 0
        up = pltpu.roll(pltpu.roll(x, 8 - s, 0), 8 * s, 1)
        down = pltpu.roll(pltpu.roll(x, s, 0), LANES - 8 * s, 1)
        x = jnp.where(odd_lane == odd_sub, x, jnp.where(odd_lane, up, down))
    out[0:8] = x[:, 0:64]
    out[8:16] = x[:, 64:128]


def analog_block(sums, **kw):
    vmem = pl.BlockSpec(memory_space=pltpu.VMEM)
    return pl.pallas_call(
        analog_kernel,
        out_shape=jax.ShapeDtypeStruct((TW, 64), jnp.float32),
        in_specs=[vmem],
        out_specs=vmem,
        compiler_params=pltpu.CompilerParams(vmem_limit_bytes=4 << 20),
        **kw,
    )(sums)


def local(
    prediction_state,
    hindcast_store,
    verifying_truth,
    quantity_factor,
    tile_day_choices,
    filled_lengths,
):
    blocks = band_blocks(
        lambda: lax.axis_index("dgrp") * DATES,
        prediction_state,
        hindcast_store,
        verifying_truth,
        quantity_factor,
        tile_day_choices,
        filled_lengths,
    )
    blocks = blocks.astype(jnp.float16)
    got = lax.all_to_all(
        blocks, "tile", split_axis=0, concat_axis=0, tiled=True, axis_index_groups=[TILE_ORDER]
    )
    sums = column_sums(got.astype(jnp.float32))
    sums = lax.all_to_all(
        sums, "dgrp", split_axis=0, concat_axis=0, tiled=True, axis_index_groups=[GROUP_ORDER]
    )
    return analog_block(sums).T


def solution(mesh):
    in_specs = (
        P(None, "tile", None),
        P("dgrp", None, "tile", None),
        P("dgrp", "tile", None),
        P(),
        P(),
        P(),
    )
    out_specs = P("dgrp", "tile")
    return jax.shard_map(local, mesh=mesh, in_specs=in_specs, out_specs=out_specs, check_vma=False)
```

```python
import functools

import jax
import jax.numpy as jnp
from jax import lax
from jax.experimental import pallas as pl
from jax.experimental.pallas import tpu as pltpu
from jax.sharding import PartitionSpec as P

DATES, QTYS, ROWS, COLS = 8, 8, 8, 1024
TILES, TW, LANES = 64, 16, 128
MAXC = 48
WAITS = {0: (0, 1, 2), 3: (3, 4, 5, 6, 7)}
FIRST_TILE = 48
TILE_ORDER = [(FIRST_TILE + i) % TILES for i in range(TILES)]
GROUP_ORDER = [6, 7, 5, 4, 3, 2, 1, 0]
GROUPS = LANES // TW

SQUARE_SCALE, MEAN_SCALE, TRUTH_SCALE = 2.0**-7, 2.0**10, 2.0**13
SMALL, LARGE_SCALE, SMALL_SCALE = 2.0**-26, 2.0**12, 2.0**41


def member_rows(base, choices, filled):
    slot = lax.broadcasted_iota(jnp.int32, (MAXC, TILES), 0)
    local = jnp.where(slot < filled, choices - base, -1)
    flags = [
        jnp.sum(jnp.where(local == d, 1.0, 0.0), axis=0, keepdims=True) for d in range(DATES)
    ]
    flags = jnp.concatenate(flags, axis=0).astype(jnp.bfloat16)
    tile = lax.broadcasted_iota(jnp.int32, (TILES, COLS), 0)
    col = lax.broadcasted_iota(jnp.int32, (TILES, COLS), 1)
    spread = jnp.where(col // TW == tile, 1.0, 0.0).astype(jnp.bfloat16)
    return jnp.dot(flags, spread, preferred_element_type=jnp.float32)


def fourth(dist9):
    base = 1.0 / (1.0 + dist9 * (1 / 9.0))
    base = base * base
    return base * base


def to_11_bits(x):
    c = x * (2.0**13 + 1)
    return c - (c - x)


def band_kernel(
    first_date,
    factor_in,
    pred_in,
    hind_in,
    truth_in,
    choices_in,
    filled_in,
    out,
    factor,
    shown,
    held,
    truth,
    choices,
    filled,
    exact,
    parts,
    sems,
):
    copies = [pltpu.make_async_copy(hind_in.at[d], held.at[d], sems.at[d]) for d in range(DATES)]
    pairs = (
        (choices_in, choices),
        (filled_in, filled),
        (pred_in, shown),
        (factor_in, factor),
        (truth_in, truth),
    )
    small = [
        pltpu.make_async_copy(src, dst, sems.at[DATES + i]) for i, (src, dst) in enumerate(pairs)
    ]
    for copy in small[:4] + copies[:1] + small[4:] + copies[1:]:
        copy.start()
    small[0].wait()
    small[1].wait()
    member = member_rows(first_date(), choices[...], filled[...])
    col = lax.broadcasted_iota(jnp.int32, (ROWS, COLS), 1)
    sub = lax.broadcasted_iota(jnp.int32, (ROWS, COLS), 0)
    small[2].wait()
    exact[...] = shown[...].astype(jnp.float32)
    small[3].wait()
    small[4].wait()
    num = jnp.zeros((ROWS, COLS), jnp.float32)
    den = jnp.zeros((ROWS, COLS), jnp.float32)
    for d in range(DATES):
        for later in WAITS.get(d, ()):
            copies[later].wait()
        err = jnp.zeros((ROWS, COLS), jnp.float32)
        for v in range(QTYS):
            dev = exact[v] - held[d, v].astype(jnp.float32)
            err = err + factor[v] * dev * dev
        left = jnp.where(col == 0, 0.0, pltpu.roll(err, 1, 1))
        right = jnp.where(col == COLS - 1, 0.0, pltpu.roll(err, COLS - 1, 1))
        side = err + left + right
        above, below = pltpu.roll(side, 1, 0), pltpu.roll(side, ROWS - 1, 0)
        flag = jnp.broadcast_to(member[d : d + 1], (ROWS, COLS))
        seen_truth = truth[d].astype(jnp.float32)
        weight = fourth(side + above + below) * flag
        num = num + weight * seen_truth
        den = den + weight
        pair = jnp.where(sub == 1, side + above, side + below)
        pair = jnp.where(flag > 0, pair * pair * SQUARE_SCALE, -1.0)
        part = jnp.where((sub == 1) | (sub == 6), pair, side * side * SQUARE_SCALE)
        scaled = seen_truth * TRUTH_SCALE
        part = jnp.where(sub == 2, pltpu.roll(scaled, 2, 0), part)
        parts[d] = jnp.where(sub == 5, pltpu.roll(scaled, ROWS - 2, 0), part)
    high = den >= SMALL
    den = to_11_bits(jnp.where(high, den * LARGE_SCALE, den * -SMALL_SCALE))
    held_den = jnp.where(high, den * (1 / LARGE_SCALE), den * (-1 / SMALL_SCALE))
    mean = jnp.where(held_den > 0, num / held_den, 0.0)
    num = mean * jnp.abs(mean) * MEAN_SCALE
    lane = lax.broadcasted_iota(jnp.int32, (ROWS, LANES), 1) // TW
    sub = lax.broadcasted_iota(jnp.int32, (ROWS, LANES), 0)
    for j in range(COLS // LANES):
        at = slice(j * LANES, (j + 1) * LANES)
        v = []
        for d in range(DATES):
            part = parts[d, :, at]
            part = jnp.where(sub == 3, pltpu.roll(num[:, at], (3 - d) % ROWS, 0), part)
            part = jnp.where(sub == 4, pltpu.roll(den[:, at], (4 - d) % ROWS, 0), part)
            v.append(part)
        for s in (1, 2, 4):
            odd = (lane & s) != 0
            for a in range(GROUPS):
                if a & s:
                    continue
                low, high = v[a], v[a | s]
                v[a] = jnp.where(odd, pltpu.roll(high, TW * s, 1), low)
                v[a | s] = jnp.where(odd, high, pltpu.roll(low, LANES - TW * s, 1))
        for t in range(GROUPS):
            out[(j * GROUPS + t - FIRST_TILE) % TILES] = v[t]


def band_blocks(first_date, prediction, hindcast, truth, factor, choices, filled, **kw):
    hbm = pl.BlockSpec(memory_space=pltpu.HBM)
    return pl.pallas_call(
        functools.partial(band_kernel, first_date),
        out_shape=jax.ShapeDtypeStruct((TILES, ROWS, LANES), jnp.float32),
        in_specs=[hbm] * 6,
        out_specs=pl.BlockSpec(memory_space=pltpu.VMEM),
        scratch_shapes=[
            pltpu.SMEM((QTYS,), jnp.float32),
            pltpu.VMEM((QTYS, ROWS, COLS), jnp.bfloat16),
            pltpu.VMEM((DATES, QTYS, ROWS, COLS), jnp.bfloat16),
            pltpu.VMEM((DATES, ROWS, COLS), jnp.bfloat16),
            pltpu.VMEM((MAXC, TILES), jnp.int32),
            pltpu.VMEM((1, TILES), jnp.int32),
            pltpu.VMEM((QTYS, ROWS, COLS), jnp.float32),
            pltpu.VMEM((DATES, ROWS, COLS), jnp.float32),
            pltpu.SemaphoreType.DMA((DATES + 5,)),
        ],
        compiler_params=pltpu.CompilerParams(vmem_limit_bytes=8 << 20),
        **kw,
    )(
        *(
            pltpu.with_memory_space_constraint(x, pltpu.HBM)
            for x in (factor, prediction, hindcast, truth, choices.T, filled[None])
        )
    )


def lane_groups_sum(x):
    for s in (4, 2, 1):
        x = x + pltpu.roll(x, TW * s, 1)
    return x


def root(x):
    x = jnp.maximum(x, 1e-30)
    inverse = lax.rsqrt(x)
    near = x * inverse
    return near + 0.5 * inverse * (x - near * near)


def rows_of_blocks(got):
    sub = lax.broadcasted_iota(jnp.int32, (ROWS, LANES), 0)
    rows = [[] for _ in range(ROWS)]
    for g in range(TILES // ROWS):
        v = [got[g * ROWS + i] for i in range(ROWS)]
        for s in (1, 2, 4):
            odd = (sub & s) != 0
            for a in range(ROWS):
                if a & s:
                    continue
                low, high = v[a], v[a | s]
                v[a] = jnp.where(odd, pltpu.roll(high, s, 0), low)
                v[a | s] = jnp.where(odd, high, pltpu.roll(low, ROWS - s, 0))
        for k in range(ROWS):
            rows[k].append(v[k])
    return [jnp.concatenate(x, axis=0) for x in rows]


def column_kernel(got, out):
    side0, pair0, truth0, mean, den, truth7, pair7, side7 = rows_of_blocks(got)
    dated0, dated7 = pair0 >= 0, pair7 >= 0
    side0, pair0, pair7, side7 = (
        root(x * (1 / SQUARE_SCALE)) for x in (side0, pair0, pair7, side7)
    )
    truth0, truth7 = truth0 * (1 / TRUTH_SCALE), truth7 * (1 / TRUTH_SCALE)
    den = jnp.where(den < 0, den * (-1 / SMALL_SCALE), den * (1 / LARGE_SCALE))
    mean_size = root(jnp.abs(mean) * (1 / MEAN_SCALE))
    num = jnp.where(mean < 0, -mean_size, mean_size) * den
    band = (lax.broadcasted_iota(jnp.int32, (TILES, LANES), 0) + FIRST_TILE) % TILES
    row = lax.broadcasted_iota(jnp.int32, (TILES, LANES), 1) // TW
    above = jnp.where(band == 0, 0.0, pltpu.roll(side7, 1, 0))
    below = jnp.where(band == TILES - 1, 0.0, pltpu.roll(side0, TILES - 1, 0))
    weight0 = jnp.where(dated0, fourth(pair0 + above), 0.0)
    weight7 = jnp.where(dated7, fourth(pair7 + below), 0.0)
    num = jnp.where(row == 0, lane_groups_sum(weight0 * truth0), num)
    num = jnp.where(row == ROWS - 1, lane_groups_sum(weight7 * truth7), num)
    den = jnp.where(row == 0, lane_groups_sum(weight0), den)
    den = jnp.where(row == ROWS - 1, lane_groups_sum(weight7), den)
    for place, g in enumerate(GROUP_ORDER):
        at = (8 * g - FIRST_TILE) % TILES
        out[place, 0:8] = num[at : at + 8]
        out[place, 8:16] = den[at : at + 8]


def column_sums(got, **kw):
    vmem = pl.BlockSpec(memory_space=pltpu.VMEM)
    return pl.pallas_call(
        column_kernel,
        out_shape=jax.ShapeDtypeStruct((8, 16, LANES), jnp.float32),
        in_specs=[vmem],
        out_specs=vmem,
        compiler_params=pltpu.CompilerParams(vmem_limit_bytes=4 << 20),
        **kw,
    )(got)


def analog_kernel(sums, out):
    total = sums[0]
    for g in range(1, 8):
        total = total + sums[g]
    analog = total[0:8] / total[8:16]
    lane = lax.broadcasted_iota(jnp.int32, (8, LANES), 1)
    sub = lax.broadcasted_iota(jnp.int32, (8, LANES), 0)
    x = jnp.take_along_axis(analog, (lane % 8) * TW + lane // 8, axis=1)
    for s in (1, 2, 4):
        odd_lane, odd_sub = ((lane // 8) & s) != 0, (sub & s) != 0
        up = pltpu.roll(pltpu.roll(x, 8 - s, 0), 8 * s, 1)
        down = pltpu.roll(pltpu.roll(x, s, 0), LANES - 8 * s, 1)
        x = jnp.where(odd_lane == odd_sub, x, jnp.where(odd_lane, up, down))
    out[0:8] = x[:, 0:64]
    out[8:16] = x[:, 64:128]


def analog_block(sums, **kw):
    vmem = pl.BlockSpec(memory_space=pltpu.VMEM)
    return pl.pallas_call(
        analog_kernel,
        out_shape=jax.ShapeDtypeStruct((TW, 64), jnp.float32),
        in_specs=[vmem],
        out_specs=vmem,
        compiler_params=pltpu.CompilerParams(vmem_limit_bytes=4 << 20),
        **kw,
    )(sums)


def local(
    prediction_state,
    hindcast_store,
    verifying_truth,
    quantity_factor,
    tile_day_choices,
    filled_lengths,
):
    blocks = band_blocks(
        lambda: lax.axis_index("dgrp") * DATES,
        prediction_state,
        hindcast_store,
        verifying_truth,
        quantity_factor,
        tile_day_choices,
        filled_lengths,
    )
    blocks = blocks.astype(jnp.float16)
    got = lax.all_to_all(
        blocks, "tile", split_axis=0, concat_axis=0, tiled=True, axis_index_groups=[TILE_ORDER]
    )
    sums = column_sums(got.astype(jnp.float32))
    sums = lax.all_to_all(
        sums, "dgrp", split_axis=0, concat_axis=0, tiled=True, axis_index_groups=[GROUP_ORDER]
    )
    return analog_block(sums).T


def solution(mesh):
    in_specs = (
        P(None, "tile", None),
        P("dgrp", None, "tile", None),
        P("dgrp", "tile", None),
        P(),
        P(),
        P(),
    )
    out_specs = P("dgrp", "tile")
    return jax.shard_map(local, mesh=mesh, in_specs=in_specs, out_specs=out_specs, check_vma=False)
```

```python
import functools

import jax
import jax.numpy as jnp
from jax import lax
from jax.experimental import pallas as pl
from jax.experimental.pallas import tpu as pltpu
from jax.sharding import PartitionSpec as P

DATES, QTYS, ROWS, COLS = 8, 8, 8, 1024
TILES, TW, LANES = 64, 16, 128
MAXC = 48
WAITS = {0: (0, 1, 2), 3: (3, 4, 5, 6, 7)}
FIRST_TILE = 48
TILE_ORDER = [(FIRST_TILE + i) % TILES for i in range(TILES)]
GROUP_ORDER = [6, 7, 5, 4, 3, 2, 1, 0]
GROUPS = LANES // TW

SQUARE_SCALE, MEAN_SCALE, TRUTH_SCALE = 2.0**-7, 2.0**10, 2.0**13
SUM_SHIFT, MEAN_SHIFT = 2.0**-3, 2.0**-11
SMALL, LARGE_SCALE, SMALL_SCALE = 2.0**-26, 2.0**12, 2.0**41


def member_rows(base, choices, filled):
    slot = lax.broadcasted_iota(jnp.int32, (MAXC, TILES), 0)
    local = jnp.where(slot < filled, choices - base, -1)
    flags = [
        jnp.sum(jnp.where(local == d, 1.0, 0.0), axis=0, keepdims=True) for d in range(DATES)
    ]
    flags = jnp.concatenate(flags, axis=0).astype(jnp.bfloat16)
    tile = lax.broadcasted_iota(jnp.int32, (TILES, COLS), 0)
    col = lax.broadcasted_iota(jnp.int32, (TILES, COLS), 1)
    spread = jnp.where(col // TW == tile, 1.0, 0.0).astype(jnp.bfloat16)
    return jnp.dot(flags, spread, preferred_element_type=jnp.float32)


def fourth(dist9):
    base = 1.0 / (1.0 + dist9 * (1 / 9.0))
    base = base * base
    return base * base


def to_11_bits(x):
    c = x * (2.0**13 + 1)
    return c - (c - x)


def band_kernel(
    first_date,
    factor_in,
    pred_in,
    hind_in,
    truth_in,
    choices_in,
    filled_in,
    out,
    factor,
    shown,
    held,
    truth,
    choices,
    filled,
    exact,
    parts,
    sems,
):
    copies = [pltpu.make_async_copy(hind_in.at[d], held.at[d], sems.at[d]) for d in range(DATES)]
    pairs = (
        (choices_in, choices),
        (filled_in, filled),
        (pred_in, shown),
        (factor_in, factor),
        (truth_in, truth),
    )
    small = [
        pltpu.make_async_copy(src, dst, sems.at[DATES + i]) for i, (src, dst) in enumerate(pairs)
    ]
    for copy in small[:4] + copies[:1] + small[4:] + copies[1:]:
        copy.start()
    small[0].wait()
    small[1].wait()
    member = member_rows(first_date(), choices[...], filled[...])
    col = lax.broadcasted_iota(jnp.int32, (ROWS, COLS), 1)
    sub = lax.broadcasted_iota(jnp.int32, (ROWS, COLS), 0)
    small[2].wait()
    exact[...] = shown[...].astype(jnp.float32)
    small[3].wait()
    small[4].wait()
    num = jnp.zeros((ROWS, COLS), jnp.float32)
    den = jnp.zeros((ROWS, COLS), jnp.float32)
    for d in range(DATES):
        for later in WAITS.get(d, ()):
            copies[later].wait()
        err = jnp.zeros((ROWS, COLS), jnp.float32)
        for v in range(QTYS):
            dev = exact[v] - held[d, v].astype(jnp.float32)
            err = err + factor[v] * dev * dev
        left = jnp.where(col == 0, 0.0, pltpu.roll(err, 1, 1))
        right = jnp.where(col == COLS - 1, 0.0, pltpu.roll(err, COLS - 1, 1))
        side = err + left + right
        above, below = pltpu.roll(side, 1, 0), pltpu.roll(side, ROWS - 1, 0)
        flag = jnp.broadcast_to(member[d : d + 1], (ROWS, COLS))
        seen_truth = truth[d].astype(jnp.float32)
        weight = fourth(side + above + below) * flag
        num = num + weight * seen_truth
        den = den + weight
        part = jnp.where(sub == 1, side + above, jnp.where(sub == 6, side + below, side)) + SUM_SHIFT
        part = part * part * SQUARE_SCALE
        part = jnp.where(((sub == 1) | (sub == 6)) & (flag == 0), -1.0, part)
        scaled = seen_truth * TRUTH_SCALE
        part = jnp.where(sub == 2, pltpu.roll(scaled, 2, 0), part)
        parts[d] = jnp.where(sub == 5, pltpu.roll(scaled, ROWS - 2, 0), part)
    high = den >= SMALL
    den = to_11_bits(jnp.where(high, den * LARGE_SCALE, den * -SMALL_SCALE))
    held_den = jnp.where(high, den * (1 / LARGE_SCALE), den * (-1 / SMALL_SCALE))
    mean = jnp.where(held_den > 0, num / held_den, 0.0)
    size = jnp.abs(mean) + MEAN_SHIFT
    size = size * size * MEAN_SCALE
    num = jnp.where(mean < 0, -size, size)
    lane = lax.broadcasted_iota(jnp.int32, (ROWS, LANES), 1) // TW
    sub = lax.broadcasted_iota(jnp.int32, (ROWS, LANES), 0)
    for j in range(COLS // LANES):
        at = slice(j * LANES, (j + 1) * LANES)
        v = []
        for d in range(DATES):
            part = parts[d, :, at]
            part = jnp.where(sub == 3, pltpu.roll(num[:, at], (3 - d) % ROWS, 0), part)
            part = jnp.where(sub == 4, pltpu.roll(den[:, at], (4 - d) % ROWS, 0), part)
            v.append(part)
        for s in (1, 2, 4):
            odd = (lane & s) != 0
            for a in range(GROUPS):
                if a & s:
                    continue
                low, high = v[a], v[a | s]
                v[a] = jnp.where(odd, pltpu.roll(high, TW * s, 1), low)
                v[a | s] = jnp.where(odd, high, pltpu.roll(low, LANES - TW * s, 1))
        for t in range(GROUPS):
            out[(j * GROUPS + t - FIRST_TILE) % TILES] = v[t]


def band_blocks(first_date, prediction, hindcast, truth, factor, choices, filled, **kw):
    hbm = pl.BlockSpec(memory_space=pltpu.HBM)
    return pl.pallas_call(
        functools.partial(band_kernel, first_date),
        out_shape=jax.ShapeDtypeStruct((TILES, ROWS, LANES), jnp.float32),
        in_specs=[hbm] * 6,
        out_specs=pl.BlockSpec(memory_space=pltpu.VMEM),
        scratch_shapes=[
            pltpu.SMEM((QTYS,), jnp.float32),
            pltpu.VMEM((QTYS, ROWS, COLS), jnp.bfloat16),
            pltpu.VMEM((DATES, QTYS, ROWS, COLS), jnp.bfloat16),
            pltpu.VMEM((DATES, ROWS, COLS), jnp.bfloat16),
            pltpu.VMEM((MAXC, TILES), jnp.int32),
            pltpu.VMEM((1, TILES), jnp.int32),
            pltpu.VMEM((QTYS, ROWS, COLS), jnp.float32),
            pltpu.VMEM((DATES, ROWS, COLS), jnp.float32),
            pltpu.SemaphoreType.DMA((DATES + 5,)),
        ],
        compiler_params=pltpu.CompilerParams(vmem_limit_bytes=8 << 20),
        **kw,
    )(
        *(
            pltpu.with_memory_space_constraint(x, pltpu.HBM)
            for x in (factor, prediction, hindcast, truth, choices.T, filled[None])
        )
    )


def lane_groups_sum(x):
    for s in (4, 2, 1):
        x = x + pltpu.roll(x, TW * s, 1)
    return x


def root(x):
    x = jnp.maximum(x, 1e-30)
    inverse = lax.rsqrt(x)
    near = x * inverse
    return near + 0.5 * inverse * (x - near * near)


def rows_of_blocks(got):
    sub = lax.broadcasted_iota(jnp.int32, (ROWS, LANES), 0)
    rows = [[] for _ in range(ROWS)]
    for g in range(TILES // ROWS):
        v = [got[g * ROWS + i] for i in range(ROWS)]
        for s in (1, 2, 4):
            odd = (sub & s) != 0
            for a in range(ROWS):
                if a & s:
                    continue
                low, high = v[a], v[a | s]
                v[a] = jnp.where(odd, pltpu.roll(high, s, 0), low)
                v[a | s] = jnp.where(odd, high, pltpu.roll(low, ROWS - s, 0))
        for k in range(ROWS):
            rows[k].append(v[k])
    return [jnp.concatenate(x, axis=0) for x in rows]


def column_kernel(got, out):
    side0, pair0, truth0, mean, den, truth7, pair7, side7 = rows_of_blocks(got)
    dated0, dated7 = pair0 >= 0, pair7 >= 0
    side0, pair0, pair7, side7 = (
        jnp.maximum(root(x * (1 / SQUARE_SCALE)) - SUM_SHIFT, 0.0)
        for x in (side0, pair0, pair7, side7)
    )
    truth0, truth7 = truth0 * (1 / TRUTH_SCALE), truth7 * (1 / TRUTH_SCALE)
    den = jnp.where(den < 0, den * (-1 / SMALL_SCALE), den * (1 / LARGE_SCALE))
    mean_size = root(jnp.abs(mean) * (1 / MEAN_SCALE)) - MEAN_SHIFT
    num = jnp.where(mean < 0, -mean_size, mean_size) * den
    band = (lax.broadcasted_iota(jnp.int32, (TILES, LANES), 0) + FIRST_TILE) % TILES
    row = lax.broadcasted_iota(jnp.int32, (TILES, LANES), 1) // TW
    above = jnp.where(band == 0, 0.0, pltpu.roll(side7, 1, 0))
    below = jnp.where(band == TILES - 1, 0.0, pltpu.roll(side0, TILES - 1, 0))
    weight0 = jnp.where(dated0, fourth(pair0 + above), 0.0)
    weight7 = jnp.where(dated7, fourth(pair7 + below), 0.0)
    num = jnp.where(row == 0, lane_groups_sum(weight0 * truth0), num)
    num = jnp.where(row == ROWS - 1, lane_groups_sum(weight7 * truth7), num)
    den = jnp.where(row == 0, lane_groups_sum(weight0), den)
    den = jnp.where(row == ROWS - 1, lane_groups_sum(weight7), den)
    for place, g in enumerate(GROUP_ORDER):
        at = (8 * g - FIRST_TILE) % TILES
        out[place, 0:8] = num[at : at + 8]
        out[place, 8:16] = den[at : at + 8]


def column_sums(got, **kw):
    vmem = pl.BlockSpec(memory_space=pltpu.VMEM)
    return pl.pallas_call(
        column_kernel,
        out_shape=jax.ShapeDtypeStruct((8, 16, LANES), jnp.float32),
        in_specs=[vmem],
        out_specs=vmem,
        compiler_params=pltpu.CompilerParams(vmem_limit_bytes=4 << 20),
        **kw,
    )(got)


def analog_kernel(sums, out):
    total = sums[0]
    for g in range(1, 8):
        total = total + sums[g]
    analog = total[0:8] / total[8:16]
    lane = lax.broadcasted_iota(jnp.int32, (8, LANES), 1)
    sub = lax.broadcasted_iota(jnp.int32, (8, LANES), 0)
    half, middle, row = lane // 64, lane // 8 % 8, lane % 8
    x = jnp.take_along_axis(analog, row * TW + half * 8 + (middle + sub) % 8, axis=1)
    x = jnp.take_along_axis(x, (sub - middle) % 8, axis=0)
    x = jnp.take_along_axis(x, half * 64 + (sub - middle) % 8 * 8 + row, axis=1)
    out[0:8] = x[:, 0:64]
    out[8:16] = x[:, 64:128]


def analog_block(sums, **kw):
    vmem = pl.BlockSpec(memory_space=pltpu.VMEM)
    return pl.pallas_call(
        analog_kernel,
        out_shape=jax.ShapeDtypeStruct((TW, 64), jnp.float32),
        in_specs=[vmem],
        out_specs=vmem,
        compiler_params=pltpu.CompilerParams(vmem_limit_bytes=4 << 20),
        **kw,
    )(sums)


def local(
    prediction_state,
    hindcast_store,
    verifying_truth,
    quantity_factor,
    tile_day_choices,
    filled_lengths,
):
    blocks = band_blocks(
        lambda: lax.axis_index("dgrp") * DATES,
        prediction_state,
        hindcast_store,
        verifying_truth,
        quantity_factor,
        tile_day_choices,
        filled_lengths,
    )
    blocks = blocks.astype(jnp.float16)
    got = lax.all_to_all(
        blocks, "tile", split_axis=0, concat_axis=0, tiled=True, axis_index_groups=[TILE_ORDER]
    )
    sums = column_sums(got.astype(jnp.float32))
    sums = lax.all_to_all(
        sums, "dgrp", split_axis=0, concat_axis=0, tiled=True, axis_index_groups=[GROUP_ORDER]
    )
    return analog_block(sums).T


def solution(mesh):
    in_specs = (
        P(None, "tile", None),
        P("dgrp", None, "tile", None),
        P("dgrp", "tile", None),
        P(),
        P(),
        P(),
    )
    out_specs = P("dgrp", "tile")
    return jax.shard_map(local, mesh=mesh, in_specs=in_specs, out_specs=out_specs, check_vma=False)
```

```python
import functools

import jax
import jax.numpy as jnp
from jax import lax
from jax.experimental import pallas as pl
from jax.experimental.pallas import tpu as pltpu
from jax.sharding import PartitionSpec as P

DATES, QTYS, ROWS, COLS = 8, 8, 8, 1024
TILES, TW, LANES = 64, 16, 128
MAXC = 48
WAITS = {0: (0, 1, 2), 3: (3, 4, 5, 6, 7)}
FIRST_TILE = 48
TILE_ORDER = [(FIRST_TILE + i) % TILES for i in range(TILES)]
GROUP_ORDER = [6, 7, 5, 4, 3, 2, 1, 0]
GROUPS = LANES // TW

SQUARE_SCALE, MEAN_SCALE, TRUTH_SCALE = 2.0**-7, 2.0**10, 2.0**13
SUM_SHIFT, MEAN_SHIFT = 2.0**-3, 2.0**-11
SMALL, LARGE_SCALE, SMALL_SCALE = 2.0**-26, 2.0**12, 2.0**41


def member_rows(base, choices, filled):
    slot = lax.broadcasted_iota(jnp.int32, (MAXC, TILES), 0)
    local = jnp.where(slot < filled, choices - base, -1)
    flags = [
        jnp.sum(jnp.where(local == d, 1.0, 0.0), axis=0, keepdims=True) for d in range(DATES)
    ]
    flags = jnp.concatenate(flags, axis=0).astype(jnp.bfloat16)
    tile = lax.broadcasted_iota(jnp.int32, (TILES, COLS), 0)
    col = lax.broadcasted_iota(jnp.int32, (TILES, COLS), 1)
    spread = jnp.where(col // TW == tile, 1.0, 0.0).astype(jnp.bfloat16)
    return jnp.dot(flags, spread, preferred_element_type=jnp.float32)


def fourth(dist9):
    base = 1.0 / (1.0 + dist9 * (1 / 9.0))
    base = base * base
    return base * base


def turned(v, place, axis, step):
    def moved(x, places):
        return pltpu.roll(x, places % 8 * step, axis) if places % 8 else x

    v = [moved(v[-i % 8], -i % 8) for i in range(8)]
    for s in (1, 2, 4):
        odd = (place & s) != 0
        v = [jnp.where(odd, v[(i - s) % 8], v[i]) for i in range(8)]
    return [moved(v[t], -t) for t in range(8)]


def to_11_bits(x):
    c = x * (2.0**13 + 1)
    return c - (c - x)


def band_kernel(
    first_date,
    factor_in,
    pred_in,
    hind_in,
    truth_in,
    choices_in,
    filled_in,
    out,
    factor,
    shown,
    held,
    truth,
    choices,
    filled,
    exact,
    parts,
    sems,
):
    copies = [pltpu.make_async_copy(hind_in.at[d], held.at[d], sems.at[d]) for d in range(DATES)]
    pairs = (
        (choices_in, choices),
        (filled_in, filled),
        (pred_in, shown),
        (factor_in, factor),
        (truth_in, truth),
    )
    small = [
        pltpu.make_async_copy(src, dst, sems.at[DATES + i]) for i, (src, dst) in enumerate(pairs)
    ]
    def start_date(d):
        for v in range(0, QTYS, 2):
            part = pl.ds(v, 2)
            pltpu.make_async_copy(hind_in.at[d, part], held.at[d, part], sems.at[d]).start()

    for copy in small[:4]:
        copy.start()
    start_date(0)
    small[4].start()
    for d in range(1, DATES):
        start_date(d)
    small[0].wait()
    small[1].wait()
    member = member_rows(first_date(), choices[...], filled[...])
    col = lax.broadcasted_iota(jnp.int32, (ROWS, COLS), 1)
    sub = lax.broadcasted_iota(jnp.int32, (ROWS, COLS), 0)
    small[2].wait()
    exact[...] = shown[...].astype(jnp.float32)
    small[3].wait()
    small[4].wait()
    num = jnp.zeros((ROWS, COLS), jnp.float32)
    den = jnp.zeros((ROWS, COLS), jnp.float32)
    for d in range(DATES):
        for later in WAITS.get(d, ()):
            copies[later].wait()
        err = jnp.zeros((ROWS, COLS), jnp.float32)
        for v in range(QTYS):
            dev = exact[v] - held[d, v].astype(jnp.float32)
            err = err + factor[v] * dev * dev
        left = jnp.where(col == 0, 0.0, pltpu.roll(err, 1, 1))
        right = jnp.where(col == COLS - 1, 0.0, pltpu.roll(err, COLS - 1, 1))
        side = err + left + right
        above, below = pltpu.roll(side, 1, 0), pltpu.roll(side, ROWS - 1, 0)
        flag = jnp.broadcast_to(member[d : d + 1], (ROWS, COLS))
        seen_truth = truth[d].astype(jnp.float32)
        weight = fourth(side + above + below) * flag
        num = num + weight * seen_truth
        den = den + weight
        part = jnp.where(sub == 1, side + above, jnp.where(sub == 6, side + below, side)) + SUM_SHIFT
        part = part * part * SQUARE_SCALE
        part = jnp.where(((sub == 1) | (sub == 6)) & (flag == 0), -1.0, part)
        scaled = seen_truth * TRUTH_SCALE
        part = jnp.where(sub == 2, pltpu.roll(scaled, 2, 0), part)
        parts[d] = jnp.where(sub == 5, pltpu.roll(scaled, ROWS - 2, 0), part)
    high = den >= SMALL
    den = to_11_bits(jnp.where(high, den * LARGE_SCALE, den * -SMALL_SCALE))
    held_den = jnp.where(high, den * (1 / LARGE_SCALE), den * (-1 / SMALL_SCALE))
    mean = jnp.where(held_den > 0, num / held_den, 0.0)
    size = jnp.abs(mean) + MEAN_SHIFT
    size = size * size * MEAN_SCALE
    num = jnp.where(mean < 0, -size, size)
    lane = lax.broadcasted_iota(jnp.int32, (ROWS, LANES), 1) // TW
    sub = lax.broadcasted_iota(jnp.int32, (ROWS, LANES), 0)
    for j in range(COLS // LANES):
        at = slice(j * LANES, (j + 1) * LANES)
        v = []
        for d in range(DATES):
            part = parts[d, :, at]
            part = jnp.where(sub == 3, pltpu.roll(num[:, at], (3 - d) % ROWS, 0), part)
            part = jnp.where(sub == 4, pltpu.roll(den[:, at], (4 - d) % ROWS, 0), part)
            v.append(part)
        v = turned(v, lane, 1, TW)
        for t in range(GROUPS):
            out[(j * GROUPS + t - FIRST_TILE) % TILES] = v[t]


def band_blocks(first_date, prediction, hindcast, truth, factor, choices, filled, **kw):
    hbm = pl.BlockSpec(memory_space=pltpu.HBM)
    return pl.pallas_call(
        functools.partial(band_kernel, first_date),
        out_shape=jax.ShapeDtypeStruct((TILES, ROWS, LANES), jnp.float32),
        in_specs=[hbm] * 6,
        out_specs=pl.BlockSpec(memory_space=pltpu.VMEM),
        scratch_shapes=[
            pltpu.SMEM((QTYS,), jnp.float32),
            pltpu.VMEM((QTYS, ROWS, COLS), jnp.bfloat16),
            pltpu.VMEM((DATES, QTYS, ROWS, COLS), jnp.bfloat16),
            pltpu.VMEM((DATES, ROWS, COLS), jnp.bfloat16),
            pltpu.VMEM((MAXC, TILES), jnp.int32),
            pltpu.VMEM((1, TILES), jnp.int32),
            pltpu.VMEM((QTYS, ROWS, COLS), jnp.float32),
            pltpu.VMEM((DATES, ROWS, COLS), jnp.float32),
            pltpu.SemaphoreType.DMA((DATES + 5,)),
        ],
        compiler_params=pltpu.CompilerParams(vmem_limit_bytes=8 << 20),
        **kw,
    )(
        *(
            pltpu.with_memory_space_constraint(x, pltpu.HBM)
            for x in (factor, prediction, hindcast, truth, choices.T, filled[None])
        )
    )


def lane_groups_sum(x):
    for s in (4, 2, 1):
        x = x + pltpu.roll(x, TW * s, 1)
    return x


def root(x):
    x = jnp.maximum(x, 1e-30)
    inverse = lax.rsqrt(x)
    near = x * inverse
    return near + 0.5 * inverse * (x - near * near)


def rows_of_blocks(got):
    sub = lax.broadcasted_iota(jnp.int32, (ROWS, LANES), 0)
    rows = [[] for _ in range(ROWS)]
    for g in range(TILES // ROWS):
        v = [got[g * ROWS + i] for i in range(ROWS)]
        v = turned(v, sub, 0, 1)
        for k in range(ROWS):
            rows[k].append(v[k])
    return [jnp.concatenate(x, axis=0) for x in rows]


def column_kernel(got, out):
    side0, pair0, truth0, mean, den, truth7, pair7, side7 = rows_of_blocks(got)
    dated0, dated7 = pair0 >= 0, pair7 >= 0
    side0, pair0, pair7, side7 = (
        jnp.maximum(root(x * (1 / SQUARE_SCALE)) - SUM_SHIFT, 0.0)
        for x in (side0, pair0, pair7, side7)
    )
    truth0, truth7 = truth0 * (1 / TRUTH_SCALE), truth7 * (1 / TRUTH_SCALE)
    den = jnp.where(den < 0, den * (-1 / SMALL_SCALE), den * (1 / LARGE_SCALE))
    mean_size = root(jnp.abs(mean) * (1 / MEAN_SCALE)) - MEAN_SHIFT
    num = jnp.where(mean < 0, -mean_size, mean_size) * den
    band = (lax.broadcasted_iota(jnp.int32, (TILES, LANES), 0) + FIRST_TILE) % TILES
    row = lax.broadcasted_iota(jnp.int32, (TILES, LANES), 1) // TW
    above = jnp.where(band == 0, 0.0, pltpu.roll(side7, 1, 0))
    below = jnp.where(band == TILES - 1, 0.0, pltpu.roll(side0, TILES - 1, 0))
    weight0 = jnp.where(dated0, fourth(pair0 + above), 0.0)
    weight7 = jnp.where(dated7, fourth(pair7 + below), 0.0)
    num = jnp.where(row == 0, lane_groups_sum(weight0 * truth0), num)
    num = jnp.where(row == ROWS - 1, lane_groups_sum(weight7 * truth7), num)
    den = jnp.where(row == 0, lane_groups_sum(weight0), den)
    den = jnp.where(row == ROWS - 1, lane_groups_sum(weight7), den)
    for place, g in enumerate(GROUP_ORDER):
        at = (8 * g - FIRST_TILE) % TILES
        out[place, 0:8] = num[at : at + 8]
        out[place, 8:16] = den[at : at + 8]


def column_sums(got, **kw):
    vmem = pl.BlockSpec(memory_space=pltpu.VMEM)
    return pl.pallas_call(
        column_kernel,
        out_shape=jax.ShapeDtypeStruct((8, 16, LANES), jnp.float32),
        in_specs=[vmem],
        out_specs=vmem,
        compiler_params=pltpu.CompilerParams(vmem_limit_bytes=4 << 20),
        **kw,
    )(got)


def analog_kernel(sums, out):
    total = sums[0]
    for g in range(1, 8):
        total = total + sums[g]
    analog = total[0:8] / total[8:16]
    lane = lax.broadcasted_iota(jnp.int32, (8, LANES), 1)
    sub = lax.broadcasted_iota(jnp.int32, (8, LANES), 0)
    half, middle, row = lane // 64, lane // 8 % 8, lane % 8
    x = jnp.take_along_axis(analog, row * TW + half * 8 + (middle + sub) % 8, axis=1)
    x = jnp.take_along_axis(x, (sub - middle) % 8, axis=0)
    x = jnp.take_along_axis(x, half * 64 + (sub - middle) % 8 * 8 + row, axis=1)
    out[0:8] = x[:, 0:64]
    out[8:16] = x[:, 64:128]


def analog_block(sums, **kw):
    vmem = pl.BlockSpec(memory_space=pltpu.VMEM)
    return pl.pallas_call(
        analog_kernel,
        out_shape=jax.ShapeDtypeStruct((TW, 64), jnp.float32),
        in_specs=[vmem],
        out_specs=vmem,
        compiler_params=pltpu.CompilerParams(vmem_limit_bytes=4 << 20),
        **kw,
    )(sums)


def local(
    prediction_state,
    hindcast_store,
    verifying_truth,
    quantity_factor,
    tile_day_choices,
    filled_lengths,
):
    blocks = band_blocks(
        lambda: lax.axis_index("dgrp") * DATES,
        prediction_state,
        hindcast_store,
        verifying_truth,
        quantity_factor,
        tile_day_choices,
        filled_lengths,
    )
    blocks = blocks.astype(jnp.float16)
    got = lax.all_to_all(
        blocks, "tile", split_axis=0, concat_axis=0, tiled=True, axis_index_groups=[TILE_ORDER]
    )
    sums = column_sums(got.astype(jnp.float32))
    sums = lax.all_to_all(
        sums, "dgrp", split_axis=0, concat_axis=0, tiled=True, axis_index_groups=[GROUP_ORDER]
    )
    return analog_block(sums).T


def solution(mesh):
    in_specs = (
        P(None, "tile", None),
        P("dgrp", None, "tile", None),
        P("dgrp", "tile", None),
        P(),
        P(),
        P(),
    )
    out_specs = P("dgrp", "tile")
    return jax.shard_map(local, mesh=mesh, in_specs=in_specs, out_specs=out_specs, check_vma=False)
```

```python
import functools

import jax
import jax.numpy as jnp
from jax import lax
from jax.experimental import pallas as pl
from jax.experimental.pallas import tpu as pltpu
from jax.sharding import PartitionSpec as P

DATES, QTYS, ROWS, COLS = 8, 8, 8, 1024
TILES, TW, LANES = 64, 16, 128
MAXC = 48
WAITS = {0: (0, 1, 2), 3: (3, 4, 5, 6, 7)}
FIRST_TILE = 48
TILE_ORDER = [(FIRST_TILE + i) % TILES for i in range(TILES)]
GROUP_ORDER = [6, 7, 5, 4, 3, 2, 1, 0]
GROUPS = LANES // TW

SQUARE_SCALE, MEAN_SCALE, TRUTH_SCALE = 2.0**-7, 2.0**10, 2.0**13
SUM_SHIFT, MEAN_SHIFT = 2.0**-3, 2.0**-11
SMALL, LARGE_SCALE, SMALL_SCALE = 2.0**-26, 2.0**12, 2.0**41


def member_rows(base, choices, filled):
    slot = lax.broadcasted_iota(jnp.int32, (MAXC, TILES), 0)
    local = jnp.where(slot < filled, choices - base, -1)
    flags = [
        jnp.sum(jnp.where(local == d, 1.0, 0.0), axis=0, keepdims=True) for d in range(DATES)
    ]
    flags = jnp.concatenate(flags, axis=0).astype(jnp.bfloat16)
    tile = lax.broadcasted_iota(jnp.int32, (TILES, COLS), 0)
    col = lax.broadcasted_iota(jnp.int32, (TILES, COLS), 1)
    spread = jnp.where(col // TW == tile, 1.0, 0.0).astype(jnp.bfloat16)
    return jnp.dot(flags, spread, preferred_element_type=jnp.float32)


def fourth(dist9):
    base = 1.0 / (1.0 + dist9 * (1 / 9.0))
    base = base * base
    return base * base


def turned(v, place, axis, step):
    def moved(x, places):
        return pltpu.roll(x, places % 8 * step, axis) if places % 8 else x

    v = [moved(v[-i % 8], -i % 8) for i in range(8)]
    for s in (1, 2, 4):
        odd = (place & s) != 0
        v = [jnp.where(odd, v[(i - s) % 8], v[i]) for i in range(8)]
    return [moved(v[t], -t) for t in range(8)]


def to_11_bits(x):
    c = x * (2.0**13 + 1)
    return c - (c - x)


def band_kernel(
    first_date,
    factor_in,
    pred_in,
    hind_in,
    truth_in,
    choices_in,
    filled_in,
    out,
    factor,
    shown,
    held,
    truth,
    choices,
    filled,
    exact,
    parts,
    sems,
):
    copies = [pltpu.make_async_copy(hind_in.at[d], held.at[d], sems.at[d]) for d in range(DATES)]
    pairs = (
        (choices_in, choices),
        (filled_in, filled),
        (pred_in, shown),
        (factor_in, factor),
        (truth_in, truth),
    )
    small = [
        pltpu.make_async_copy(src, dst, sems.at[DATES + i]) for i, (src, dst) in enumerate(pairs)
    ]
    def start_date(d):
        for v in range(0, QTYS, 2):
            part = pl.ds(v, 2)
            pltpu.make_async_copy(hind_in.at[d, part], held.at[d, part], sems.at[d]).start()

    for copy in small[:2] + small[3:4]:
        copy.start()
    for v in range(0, QTYS, 2):
        part = pl.ds(v, 2)
        pltpu.make_async_copy(pred_in.at[part], shown.at[part], sems.at[DATES + 2]).start()
    start_date(0)
    small[4].start()
    for d in range(1, DATES):
        start_date(d)
    small[0].wait()
    small[1].wait()
    member = member_rows(first_date(), choices[...], filled[...])
    col = lax.broadcasted_iota(jnp.int32, (ROWS, COLS), 1)
    sub = lax.broadcasted_iota(jnp.int32, (ROWS, COLS), 0)
    small[2].wait()
    exact[...] = shown[...].astype(jnp.float32)
    small[3].wait()
    small[4].wait()
    num = jnp.zeros((ROWS, COLS), jnp.float32)
    den = jnp.zeros((ROWS, COLS), jnp.float32)
    for d in range(DATES):
        for later in WAITS.get(d, ()):
            copies[later].wait()
        err = jnp.zeros((ROWS, COLS), jnp.float32)
        for v in range(QTYS):
            dev = exact[v] - held[d, v].astype(jnp.float32)
            err = err + factor[v] * dev * dev
        left = jnp.where(col == 0, 0.0, pltpu.roll(err, 1, 1))
        right = jnp.where(col == COLS - 1, 0.0, pltpu.roll(err, COLS - 1, 1))
        side = err + left + right
        above, below = pltpu.roll(side, 1, 0), pltpu.roll(side, ROWS - 1, 0)
        flag = jnp.broadcast_to(member[d : d + 1], (ROWS, COLS))
        seen_truth = truth[d].astype(jnp.float32)
        weight = fourth(side + above + below) * flag
        num = num + weight * seen_truth
        den = den + weight
        part = jnp.where(sub == 1, side + above, jnp.where(sub == 6, side + below, side)) + SUM_SHIFT
        part = part * part * SQUARE_SCALE
        part = jnp.where(((sub == 1) | (sub == 6)) & (flag == 0), -1.0, part)
        scaled = seen_truth * TRUTH_SCALE
        part = jnp.where(sub == 2, pltpu.roll(scaled, 2, 0), part)
        parts[d] = jnp.where(sub == 5, pltpu.roll(scaled, ROWS - 2, 0), part)
    high = den >= SMALL
    den = to_11_bits(jnp.where(high, den * LARGE_SCALE, den * -SMALL_SCALE))
    held_den = jnp.where(high, den * (1 / LARGE_SCALE), den * (-1 / SMALL_SCALE))
    mean = jnp.where(held_den > 0, num / held_den, 0.0)
    size = jnp.abs(mean) + MEAN_SHIFT
    size = size * size * MEAN_SCALE
    num = jnp.where(mean < 0, -size, size)
    lane = lax.broadcasted_iota(jnp.int32, (ROWS, LANES), 1) // TW
    sub = lax.broadcasted_iota(jnp.int32, (ROWS, LANES), 0)
    for j in range(COLS // LANES):
        at = slice(j * LANES, (j + 1) * LANES)
        v = []
        for d in range(DATES):
            part = parts[d, :, at]
            part = jnp.where(sub == 3, pltpu.roll(num[:, at], (3 - d) % ROWS, 0), part)
            part = jnp.where(sub == 4, pltpu.roll(den[:, at], (4 - d) % ROWS, 0), part)
            v.append(part)
        v = turned(v, lane, 1, TW)
        for t in range(GROUPS):
            out[(j * GROUPS + t - FIRST_TILE) % TILES] = v[t]


def band_blocks(first_date, prediction, hindcast, truth, factor, choices, filled, **kw):
    hbm = pl.BlockSpec(memory_space=pltpu.HBM)
    return pl.pallas_call(
        functools.partial(band_kernel, first_date),
        out_shape=jax.ShapeDtypeStruct((TILES, ROWS, LANES), jnp.float32),
        in_specs=[hbm] * 6,
        out_specs=pl.BlockSpec(memory_space=pltpu.VMEM),
        scratch_shapes=[
            pltpu.SMEM((QTYS,), jnp.float32),
            pltpu.VMEM((QTYS, ROWS, COLS), jnp.bfloat16),
            pltpu.VMEM((DATES, QTYS, ROWS, COLS), jnp.bfloat16),
            pltpu.VMEM((DATES, ROWS, COLS), jnp.bfloat16),
            pltpu.VMEM((MAXC, TILES), jnp.int32),
            pltpu.VMEM((1, TILES), jnp.int32),
            pltpu.VMEM((QTYS, ROWS, COLS), jnp.float32),
            pltpu.VMEM((DATES, ROWS, COLS), jnp.float32),
            pltpu.SemaphoreType.DMA((DATES + 5,)),
        ],
        compiler_params=pltpu.CompilerParams(vmem_limit_bytes=8 << 20),
        **kw,
    )(
        *(
            pltpu.with_memory_space_constraint(x, pltpu.HBM)
            for x in (factor, prediction, hindcast, truth, choices.T, filled[None])
        )
    )


def lane_groups_sum(x):
    for s in (4, 2, 1):
        x = x + pltpu.roll(x, TW * s, 1)
    return x


def root(x):
    x = jnp.maximum(x, 1e-30)
    inverse = lax.rsqrt(x)
    near = x * inverse
    return near + 0.5 * inverse * (x - near * near)


def rows_of_blocks(got):
    sub = lax.broadcasted_iota(jnp.int32, (ROWS, LANES), 0)
    rows = [[] for _ in range(ROWS)]
    for g in range(TILES // ROWS):
        v = [got[g * ROWS + i] for i in range(ROWS)]
        v = turned(v, sub, 0, 1)
        for k in range(ROWS):
            rows[k].append(v[k])
    return [jnp.concatenate(x, axis=0) for x in rows]


def column_kernel(got, out):
    side0, pair0, truth0, mean, den, truth7, pair7, side7 = rows_of_blocks(got)
    dated0, dated7 = pair0 >= 0, pair7 >= 0
    side0, pair0, pair7, side7 = (
        jnp.maximum(root(x * (1 / SQUARE_SCALE)) - SUM_SHIFT, 0.0)
        for x in (side0, pair0, pair7, side7)
    )
    truth0, truth7 = truth0 * (1 / TRUTH_SCALE), truth7 * (1 / TRUTH_SCALE)
    den = jnp.where(den < 0, den * (-1 / SMALL_SCALE), den * (1 / LARGE_SCALE))
    mean_size = root(jnp.abs(mean) * (1 / MEAN_SCALE)) - MEAN_SHIFT
    num = jnp.where(mean < 0, -mean_size, mean_size) * den
    band = (lax.broadcasted_iota(jnp.int32, (TILES, LANES), 0) + FIRST_TILE) % TILES
    row = lax.broadcasted_iota(jnp.int32, (TILES, LANES), 1) // TW
    above = jnp.where(band == 0, 0.0, pltpu.roll(side7, 1, 0))
    below = jnp.where(band == TILES - 1, 0.0, pltpu.roll(side0, TILES - 1, 0))
    weight0 = jnp.where(dated0, fourth(pair0 + above), 0.0)
    weight7 = jnp.where(dated7, fourth(pair7 + below), 0.0)
    num = jnp.where(row == 0, lane_groups_sum(weight0 * truth0), num)
    num = jnp.where(row == ROWS - 1, lane_groups_sum(weight7 * truth7), num)
    den = jnp.where(row == 0, lane_groups_sum(weight0), den)
    den = jnp.where(row == ROWS - 1, lane_groups_sum(weight7), den)
    for place, g in enumerate(GROUP_ORDER):
        at = (8 * g - FIRST_TILE) % TILES
        out[place, 0:8] = num[at : at + 8]
        out[place, 8:16] = den[at : at + 8]


def column_sums(got, **kw):
    vmem = pl.BlockSpec(memory_space=pltpu.VMEM)
    return pl.pallas_call(
        column_kernel,
        out_shape=jax.ShapeDtypeStruct((8, 16, LANES), jnp.float32),
        in_specs=[vmem],
        out_specs=vmem,
        compiler_params=pltpu.CompilerParams(vmem_limit_bytes=4 << 20),
        **kw,
    )(got)


def analog_kernel(sums, out):
    total = sums[0]
    for g in range(1, 8):
        total = total + sums[g]
    analog = total[0:8] / total[8:16]
    lane = lax.broadcasted_iota(jnp.int32, (8, LANES), 1)
    sub = lax.broadcasted_iota(jnp.int32, (8, LANES), 0)
    half, middle, row = lane // 64, lane // 8 % 8, lane % 8
    x = jnp.take_along_axis(analog, row * TW + half * 8 + (middle + sub) % 8, axis=1)
    x = jnp.take_along_axis(x, (sub - middle) % 8, axis=0)
    x = jnp.take_along_axis(x, half * 64 + (sub - middle) % 8 * 8 + row, axis=1)
    out[0:8] = x[:, 0:64]
    out[8:16] = x[:, 64:128]


def analog_block(sums, **kw):
    vmem = pl.BlockSpec(memory_space=pltpu.VMEM)
    return pl.pallas_call(
        analog_kernel,
        out_shape=jax.ShapeDtypeStruct((TW, 64), jnp.float32),
        in_specs=[vmem],
        out_specs=vmem,
        compiler_params=pltpu.CompilerParams(vmem_limit_bytes=4 << 20),
        **kw,
    )(sums)


def local(
    prediction_state,
    hindcast_store,
    verifying_truth,
    quantity_factor,
    tile_day_choices,
    filled_lengths,
):
    blocks = band_blocks(
        lambda: lax.axis_index("dgrp") * DATES,
        prediction_state,
        hindcast_store,
        verifying_truth,
        quantity_factor,
        tile_day_choices,
        filled_lengths,
    )
    blocks = blocks.astype(jnp.float16)
    got = lax.all_to_all(
        blocks, "tile", split_axis=0, concat_axis=0, tiled=True, axis_index_groups=[TILE_ORDER]
    )
    sums = column_sums(got.astype(jnp.float32))
    sums = lax.all_to_all(
        sums, "dgrp", split_axis=0, concat_axis=0, tiled=True, axis_index_groups=[GROUP_ORDER]
    )
    return analog_block(sums).T


def solution(mesh):
    in_specs = (
        P(None, "tile", None),
        P("dgrp", None, "tile", None),
        P("dgrp", "tile", None),
        P(),
        P(),
        P(),
    )
    out_specs = P("dgrp", "tile")
    return jax.shard_map(local, mesh=mesh, in_specs=in_specs, out_specs=out_specs, check_vma=False)
```

```python
import functools

import jax
import jax.numpy as jnp
from jax import lax
from jax.experimental import pallas as pl
from jax.experimental.pallas import tpu as pltpu
from jax.sharding import PartitionSpec as P

DATES, QTYS, ROWS, COLS = 8, 8, 8, 1024
TILES, TW, LANES = 64, 16, 128
MAXC = 48
WAITS = {0: (0, 1, 2), 3: (3, 4, 5, 6, 7)}
FIRST_TILE = 48
TILE_ORDER = [(FIRST_TILE + i) % TILES for i in range(TILES)]
GROUP_ORDER = [7, 6, 5, 4, 3, 2, 1, 0]
GROUPS = LANES // TW

SQUARE_SCALE, MEAN_SCALE, TRUTH_SCALE = 2.0**-7, 2.0**10, 2.0**13
SUM_SHIFT, MEAN_SHIFT = 2.0**-3, 2.0**-11
SMALL, LARGE_SCALE, SMALL_SCALE = 2.0**-26, 2.0**12, 2.0**41


def member_rows(base, choices, filled):
    slot = lax.broadcasted_iota(jnp.int32, (MAXC, TILES), 0)
    local = jnp.where(slot < filled, choices - base, -1)
    flags = [
        jnp.sum(jnp.where(local == d, 1.0, 0.0), axis=0, keepdims=True) for d in range(DATES)
    ]
    flags = jnp.concatenate(flags, axis=0).astype(jnp.bfloat16)
    tile = lax.broadcasted_iota(jnp.int32, (TILES, COLS), 0)
    col = lax.broadcasted_iota(jnp.int32, (TILES, COLS), 1)
    spread = jnp.where(col // TW == tile, 1.0, 0.0).astype(jnp.bfloat16)
    return jnp.dot(flags, spread, preferred_element_type=jnp.float32)


def fourth(dist9):
    base = 1.0 / (1.0 + dist9 * (1 / 9.0))
    base = base * base
    return base * base


def turned(v, place, axis, step):
    def moved(x, places):
        return pltpu.roll(x, places % 8 * step, axis) if places % 8 else x

    v = [moved(v[-i % 8], -i % 8) for i in range(8)]
    for s in (1, 2, 4):
        odd = (place & s) != 0
        v = [jnp.where(odd, v[(i - s) % 8], v[i]) for i in range(8)]
    return [moved(v[t], -t) for t in range(8)]


def to_11_bits(x):
    c = x * (2.0**13 + 1)
    return c - (c - x)


def band_kernel(
    first_date,
    factor_in,
    pred_in,
    hind_in,
    truth_in,
    choices_in,
    filled_in,
    out,
    factor,
    shown,
    held,
    truth,
    choices,
    filled,
    exact,
    parts,
    sems,
):
    copies = [pltpu.make_async_copy(hind_in.at[d], held.at[d], sems.at[d]) for d in range(DATES)]
    pairs = (
        (choices_in, choices),
        (filled_in, filled),
        (pred_in, shown),
        (factor_in, factor),
        (truth_in, truth),
    )
    small = [
        pltpu.make_async_copy(src, dst, sems.at[DATES + i]) for i, (src, dst) in enumerate(pairs)
    ]
    def start_date(d):
        for v in range(0, QTYS, 2):
            part = pl.ds(v, 2)
            pltpu.make_async_copy(hind_in.at[d, part], held.at[d, part], sems.at[d]).start()

    for copy in small[:2] + small[3:4]:
        copy.start()
    for v in range(0, QTYS, 2):
        part = pl.ds(v, 2)
        pltpu.make_async_copy(pred_in.at[part], shown.at[part], sems.at[DATES + 2]).start()
    start_date(0)
    small[4].start()
    for d in range(1, DATES):
        start_date(d)
    small[0].wait()
    small[1].wait()
    member = member_rows(first_date(), choices[...], filled[...])
    col = lax.broadcasted_iota(jnp.int32, (ROWS, COLS), 1)
    sub = lax.broadcasted_iota(jnp.int32, (ROWS, COLS), 0)
    small[2].wait()
    exact[...] = shown[...].astype(jnp.float32)
    small[3].wait()
    small[4].wait()
    num = jnp.zeros((ROWS, COLS), jnp.float32)
    den = jnp.zeros((ROWS, COLS), jnp.float32)
    for d in range(DATES):
        for later in WAITS.get(d, ()):
            copies[later].wait()
        err = jnp.zeros((ROWS, COLS), jnp.float32)
        for v in range(QTYS):
            dev = exact[v] - held[d, v].astype(jnp.float32)
            err = err + factor[v] * dev * dev
        left = jnp.where(col == 0, 0.0, pltpu.roll(err, 1, 1))
        right = jnp.where(col == COLS - 1, 0.0, pltpu.roll(err, COLS - 1, 1))
        side = err + left + right
        above, below = pltpu.roll(side, 1, 0), pltpu.roll(side, ROWS - 1, 0)
        flag = jnp.broadcast_to(member[d : d + 1], (ROWS, COLS))
        seen_truth = truth[d].astype(jnp.float32)
        weight = fourth(side + above + below) * flag
        num = num + weight * seen_truth
        den = den + weight
        part = jnp.where(sub == 1, side + above, jnp.where(sub == 6, side + below, side)) + SUM_SHIFT
        part = part * part * SQUARE_SCALE
        part = jnp.where(((sub == 1) | (sub == 6)) & (flag == 0), -1.0, part)
        scaled = seen_truth * TRUTH_SCALE
        part = jnp.where(sub == 2, pltpu.roll(scaled, 2, 0), part)
        parts[d] = jnp.where(sub == 5, pltpu.roll(scaled, ROWS - 2, 0), part)
    high = den >= SMALL
    den = to_11_bits(jnp.where(high, den * LARGE_SCALE, den * -SMALL_SCALE))
    held_den = jnp.where(high, den * (1 / LARGE_SCALE), den * (-1 / SMALL_SCALE))
    mean = jnp.where(held_den > 0, num / held_den, 0.0)
    size = jnp.abs(mean) + MEAN_SHIFT
    size = size * size * MEAN_SCALE
    num = jnp.where(mean < 0, -size, size)
    lane = lax.broadcasted_iota(jnp.int32, (ROWS, LANES), 1) // TW
    sub = lax.broadcasted_iota(jnp.int32, (ROWS, LANES), 0)
    for j in range(COLS // LANES):
        at = slice(j * LANES, (j + 1) * LANES)
        v = []
        for d in range(DATES):
            part = parts[d, :, at]
            part = jnp.where(sub == 3, pltpu.roll(num[:, at], (3 - d) % ROWS, 0), part)
            part = jnp.where(sub == 4, pltpu.roll(den[:, at], (4 - d) % ROWS, 0), part)
            v.append(part)
        v = turned(v, lane, 1, TW)
        for t in range(GROUPS):
            out[(j * GROUPS + t - FIRST_TILE) % TILES] = v[t]


def band_blocks(first_date, prediction, hindcast, truth, factor, choices, filled, **kw):
    hbm = pl.BlockSpec(memory_space=pltpu.HBM)
    return pl.pallas_call(
        functools.partial(band_kernel, first_date),
        out_shape=jax.ShapeDtypeStruct((TILES, ROWS, LANES), jnp.float32),
        in_specs=[hbm] * 6,
        out_specs=pl.BlockSpec(memory_space=pltpu.VMEM),
        scratch_shapes=[
            pltpu.SMEM((QTYS,), jnp.float32),
            pltpu.VMEM((QTYS, ROWS, COLS), jnp.bfloat16),
            pltpu.VMEM((DATES, QTYS, ROWS, COLS), jnp.bfloat16),
            pltpu.VMEM((DATES, ROWS, COLS), jnp.bfloat16),
            pltpu.VMEM((MAXC, TILES), jnp.int32),
            pltpu.VMEM((1, TILES), jnp.int32),
            pltpu.VMEM((QTYS, ROWS, COLS), jnp.float32),
            pltpu.VMEM((DATES, ROWS, COLS), jnp.float32),
            pltpu.SemaphoreType.DMA((DATES + 5,)),
        ],
        compiler_params=pltpu.CompilerParams(vmem_limit_bytes=8 << 20),
        **kw,
    )(
        *(
            pltpu.with_memory_space_constraint(x, pltpu.HBM)
            for x in (factor, prediction, hindcast, truth, choices.T, filled[None])
        )
    )


def lane_groups_sum(x):
    for s in (4, 2, 1):
        x = x + pltpu.roll(x, TW * s, 1)
    return x


def root(x):
    x = jnp.maximum(x, 1e-30)
    inverse = lax.rsqrt(x)
    near = x * inverse
    return near + 0.5 * inverse * (x - near * near)


def rows_of_blocks(got):
    sub = lax.broadcasted_iota(jnp.int32, (ROWS, LANES), 0)
    rows = [[] for _ in range(ROWS)]
    for g in range(TILES // ROWS):
        v = [got[g * ROWS + i] for i in range(ROWS)]
        v = turned(v, sub, 0, 1)
        for k in range(ROWS):
            rows[k].append(v[k])
    return [jnp.concatenate(x, axis=0) for x in rows]


def column_kernel(got, out):
    side0, pair0, truth0, mean, den, truth7, pair7, side7 = rows_of_blocks(got)
    dated0, dated7 = pair0 >= 0, pair7 >= 0
    side0, pair0, pair7, side7 = (
        jnp.maximum(root(x * (1 / SQUARE_SCALE)) - SUM_SHIFT, 0.0)
        for x in (side0, pair0, pair7, side7)
    )
    truth0, truth7 = truth0 * (1 / TRUTH_SCALE), truth7 * (1 / TRUTH_SCALE)
    den = jnp.where(den < 0, den * (-1 / SMALL_SCALE), den * (1 / LARGE_SCALE))
    mean_size = root(jnp.abs(mean) * (1 / MEAN_SCALE)) - MEAN_SHIFT
    num = jnp.where(mean < 0, -mean_size, mean_size) * den
    band = (lax.broadcasted_iota(jnp.int32, (TILES, LANES), 0) + FIRST_TILE) % TILES
    row = lax.broadcasted_iota(jnp.int32, (TILES, LANES), 1) // TW
    above = jnp.where(band == 0, 0.0, pltpu.roll(side7, 1, 0))
    below = jnp.where(band == TILES - 1, 0.0, pltpu.roll(side0, TILES - 1, 0))
    weight0 = jnp.where(dated0, fourth(pair0 + above), 0.0)
    weight7 = jnp.where(dated7, fourth(pair7 + below), 0.0)
    num = jnp.where(row == 0, lane_groups_sum(weight0 * truth0), num)
    num = jnp.where(row == ROWS - 1, lane_groups_sum(weight7 * truth7), num)
    den = jnp.where(row == 0, lane_groups_sum(weight0), den)
    den = jnp.where(row == ROWS - 1, lane_groups_sum(weight7), den)
    for place, g in enumerate(GROUP_ORDER):
        at = (8 * g - FIRST_TILE) % TILES
        out[place, 0:8] = num[at : at + 8]
        out[place, 8:16] = den[at : at + 8]


def column_sums(got, **kw):
    vmem = pl.BlockSpec(memory_space=pltpu.VMEM)
    return pl.pallas_call(
        column_kernel,
        out_shape=jax.ShapeDtypeStruct((8, 16, LANES), jnp.float32),
        in_specs=[vmem],
        out_specs=vmem,
        compiler_params=pltpu.CompilerParams(vmem_limit_bytes=4 << 20),
        **kw,
    )(got)


def analog_kernel(sums, out):
    total = sums[0]
    for g in range(1, 8):
        total = total + sums[g]
    analog = total[0:8] / total[8:16]
    lane = lax.broadcasted_iota(jnp.int32, (8, LANES), 1)
    sub = lax.broadcasted_iota(jnp.int32, (8, LANES), 0)
    half, middle, row = lane // 64, lane // 8 % 8, lane % 8
    x = jnp.take_along_axis(analog, row * TW + half * 8 + (middle + sub) % 8, axis=1)
    x = jnp.take_along_axis(x, (sub - middle) % 8, axis=0)
    x = jnp.take_along_axis(x, half * 64 + (sub - middle) % 8 * 8 + row, axis=1)
    out[0:8] = x[:, 0:64]
    out[8:16] = x[:, 64:128]


def analog_block(sums, **kw):
    vmem = pl.BlockSpec(memory_space=pltpu.VMEM)
    return pl.pallas_call(
        analog_kernel,
        out_shape=jax.ShapeDtypeStruct((TW, 64), jnp.float32),
        in_specs=[vmem],
        out_specs=vmem,
        compiler_params=pltpu.CompilerParams(vmem_limit_bytes=4 << 20),
        **kw,
    )(sums)


def local(
    prediction_state,
    hindcast_store,
    verifying_truth,
    quantity_factor,
    tile_day_choices,
    filled_lengths,
):
    blocks = band_blocks(
        lambda: lax.axis_index("dgrp") * DATES,
        prediction_state,
        hindcast_store,
        verifying_truth,
        quantity_factor,
        tile_day_choices,
        filled_lengths,
    )
    blocks = blocks.astype(jnp.float16)
    got = lax.all_to_all(
        blocks, "tile", split_axis=0, concat_axis=0, tiled=True, axis_index_groups=[TILE_ORDER]
    )
    sums = column_sums(got.astype(jnp.float32))
    sums = lax.all_to_all(
        sums, "dgrp", split_axis=0, concat_axis=0, tiled=True, axis_index_groups=[GROUP_ORDER]
    )
    return analog_block(sums).T


def solution(mesh):
    in_specs = (
        P(None, "tile", None),
        P("dgrp", None, "tile", None),
        P("dgrp", "tile", None),
        P(),
        P(),
        P(),
    )
    out_specs = P("dgrp", "tile")
    return jax.shard_map(local, mesh=mesh, in_specs=in_specs, out_specs=out_specs, check_vma=False)
```
